256 devices in a mesh: dp: 8 (over y, core), tm: 32 (over z, x).
Axes of the slice: x: 4, y: 4, z: 8, core: 2. Of those that a mesh axis runs over, the one named last changes fastest.
Arguments:
- frames: bfloat16 [65536, 1536], P(('dp', 'tm')), may hold values from -28 to 28, as said below
- seg: int32 [8, 8192], P('dp'), may hold values from 0 to 3, never falling along the last dimension, each value on 1 to 4096 neighbouring positions
- look_back: int32 [8, 32], P('dp'), may hold values 0 or 1
- w_dw: float32 [5, 1536], replicated, may hold values from -2.5 to 2.5
- w_qkv: bfloat16 [1536, 4608], P(None, 'dp'), may hold values from -0.15625 to 0.15625
- w_o: bfloat16 [1536, 1536], replicated, may hold values from -1.5 to 1.5
- cotangent: bfloat16 [65536, 1536], P(('dp', 'tm')), may hold values from -1 to 1
Outputs:
- mixed: bfloat16 [65536, 1536], P(('dp', 'tm'))
- weight_grad: float32 [1536, 1536], P('tm', 'dp')
The draws below stay inside these ranges and needn't reach their ends.
Inputs may be any that keep to these rules, and one draw needn't show every extreme that they name: Float features; a few short runs of frames may be several times larger than the rest. `seg`: recording numbers never fall along a replica's frames; each recording has 1 to 4096 frames, one exactly 4096.
All inputs are finite; a program needn't handle non-finite values. No bound on the sum of `look_back` on one device may be relied on, other than what follows from the above.
Results may differ from the reference program's by a relative error of at most 0.012.
The reference program's roundings to bfloat16 on the way count: a program that leaves them out, or rounds other values in their place, can miss the bound.
Values may be sent and summed in bfloat16 or wider, within the bound.
A program may use at most 128 MiB of HBM per device.

```python
import math
import jax
import jax.numpy as jnp
import numpy as np
from jax import lax

D = 1536
HEADS = 16
KER = 5
HDIM = 96
STRETCH = 256
REC = 4
FR = 8192
FRAMES = 65536
NCH = 32
MOST = 4096
N_DP = 8


def draw_frames(key, part):
    first_key = jax.random.fold_in(key, 0)
    values = jnp.clip(jax.random.normal(first_key, (FRAMES, D), jnp.float32), -6.0, 6.0)
    return values.astype(jnp.bfloat16)


def plant(values, key, smallest, largest):
    dims = values.shape
    index_at = [jax.random.randint(jax.random.fold_in(key, axis), (), 0, dims[axis]) for axis in range(len(dims))]
    values = values.at[tuple(index_at)].set(smallest)
    longest = dims.index(max(dims))
    index_at[longest] = (index_at[longest] + 1) % dims[longest]
    return values.at[tuple(index_at)].set(largest)


def spiked(values, own_key, source, target, blocks, factor):
    owner, partner = [(jnp.arange(values.shape[dim]) // (values.shape[dim] // blocks)).reshape([-1 if axis == dim else 1 for axis in range(values.ndim)]) for dim in (source, target)]
    chosen = jax.random.permutation(own_key, blocks)[partner]
    strong = (owner == chosen) | (owner == (partner + blocks // 2) % blocks)
    return jnp.where(strong, factor * values, values)


def steps_of(rng, dims, pieces, smallest, top_value):
    gain, own = 1.0, jax.random.fold_in(rng, 6)
    for axis_at, shards_of in pieces:
        draws = jnp.exp(jax.random.uniform(jax.random.fold_in(own, axis_at), (shards_of,), jnp.float32, smallest / len(pieces), top_value / len(pieces)))
        gain = gain * jnp.repeat(draws, dims[axis_at] // shards_of).reshape([-1 if axis == axis_at else 1 for axis in range(len(dims))])
    return gain


def length_profile(count, total, bound, lean):
    loads = [(1 << 20) // math.isqrt(grade ** lean) + 1 for grade in range(2, count + 1)]
    spare, holding = total - bound - (count - 1), [1] * (count - 1)
    while spare > 0:
        movable = [i for i in range(count - 1) if holding[i] < bound]
        pool, remaining = sum([loads[i] for i in movable]), spare
        for i in movable:
            addition = min(bound - holding[i], max(1, remaining * loads[i] // pool), spare)
            holding[i] = holding[i] + addition
            spare = spare - addition
    return np.array([bound] + holding)


def ragged_sizes(rng, count, total, bound, skew):
    if count == 2:
        one = jax.random.randint(rng, (), max(1, total - bound), min(bound, total - 1) + 1)
        return jnp.stack([one, total - one])
    sizes = jnp.asarray(length_profile(count, total, bound, skew), jnp.int32)
    twos = (count - 1) // 2
    giver, sink = sizes[1:1 + 2 * twos:2], sizes[2:2 + 2 * twos:2]
    margin = jnp.minimum(giver - 1, bound - sink)
    shifted = jax.random.randint(jax.random.fold_in(rng, 1), (twos,), 0, 1 << 20) % (margin + 1)
    sizes = sizes.at[1:1 + 2 * twos:2].set(giver - shifted).at[2:2 + 2 * twos:2].set(sink + shifted)
    return sizes[jax.random.permutation(jax.random.fold_in(rng, 2), count)]


def bell_draw(own_key, shape, scale, bound, cuts=(), kind=jnp.bfloat16):
    values = jax.random.normal(own_key, shape, jnp.float32) * scale
    if len(cuts) > 0:
        values = steps_of(own_key, shape, cuts, -0.22, 0.18) * values
    return jnp.clip(values, min=-bound, max=bound).astype(kind)


def heavy_noise(own_key, extent, deviation, limit, cuts, heavy, held_as=jnp.bfloat16):
    drawn = deviation * jax.random.normal(own_key, extent, jnp.float32)
    if cuts:
        drawn = drawn * steps_of(own_key, extent, cuts, -0.22, 0.18)
    return jnp.clip(spiked(drawn, jax.random.fold_in(own_key, 3), *heavy), -limit, limit).astype(held_as)


def setup_inputs(seed: int = 0) -> dict:
    arg_keys = jax.random.split(jax.random.key(seed), 8)
    frames = draw_frames(jax.random.fold_in(arg_keys[7], 71), 0)
    seg = jax.vmap(lambda own: jnp.searchsorted(jnp.cumsum(ragged_sizes(own, REC, FR, MOST, 1)), jnp.arange(FR), side="right"))(jax.random.split(arg_keys[1], N_DP)).reshape((N_DP, FR)).astype(jnp.int32)
    look_back = plant((jax.random.randint(arg_keys[2], (N_DP, NCH), 0, 4) < 3).astype(jnp.int32), jax.random.fold_in(arg_keys[2], 1), 0, 1)
    w_dw = bell_draw(arg_keys[3], (KER, D), KER ** -0.5, 2.5, (), jnp.float32)
    w_qkv = bell_draw(arg_keys[4], (D, 3 * D), D ** -0.5, 0.15625, ((1, 8),))
    w_o = bell_draw(arg_keys[5], (D, D), 16 ** -0.5, 1.5)
    cotangent = heavy_noise(arg_keys[6], (FRAMES, D), 0.04, 1.0, ((0, 256),), (0, 1, 256, 6.0))
    return dict(frames=frames, seg=seg, look_back=look_back, w_dw=w_dw, w_qkv=w_qkv, w_o=w_o, cotangent=cotangent)


def stretch_attention(queries, keys, values, seg_row, look_row, stretch):
    frame_count, heads_here, head_dim = queries.shape
    value_dim = values.shape[2]
    blocks = frame_count // stretch
    query_blocks = queries.reshape(blocks, stretch, heads_here, head_dim)
    key_blocks = keys.reshape(blocks, stretch, heads_here, head_dim)
    value_blocks = values.reshape(blocks, stretch, heads_here, value_dim)
    key_pairs = jnp.concatenate([jnp.concatenate([jnp.zeros_like(key_blocks[:1]), key_blocks[:-1]], 0), key_blocks], 1)
    value_pairs = jnp.concatenate([jnp.concatenate([jnp.zeros_like(value_blocks[:1]), value_blocks[:-1]], 0), value_blocks], 1)
    seg_blocks = seg_row.reshape(blocks, stretch)
    seg_pairs = jnp.concatenate([jnp.concatenate([jnp.full((1, stretch), -1, jnp.int32), seg_blocks[:-1]], 0), seg_blocks], 1)
    allow_prev = look_row == 1
    per_step = math.gcd(blocks, max(1, 512 // stretch))
    current = jnp.arange(2 * stretch) >= stretch
    scale = 1.0 / math.sqrt(head_dim)

    def block_step(block_index):
        start = (block_index * per_step).astype(jnp.int32)

        def pick_rows(array):
            return lax.dynamic_slice_in_dim(array, start, per_step, 0)
        scores = jnp.einsum('gqhd,gkhd->ghqk', pick_rows(query_blocks).astype(jnp.float32), pick_rows(key_pairs).astype(jnp.float32)) * scale
        same_rec = pick_rows(seg_pairs)[:, None, :] == pick_rows(seg_blocks)[:, :, None]
        allowed = same_rec & (current[None, None, :] | pick_rows(allow_prev)[:, None, None])
        scores = jnp.where(allowed[:, None], scores, -1e+30)
        row_max = lax.optimization_barrier(jnp.max(scores, axis=-1, keepdims=True))
        raw_weights = jnp.exp(scores - row_max)
        probs = (raw_weights / lax.optimization_barrier(jnp.sum(raw_weights, axis=-1, keepdims=True))).astype(jnp.bfloat16)
        outputs = jnp.einsum('ghqk,gkhv->gqhv', probs.astype(jnp.float32), pick_rows(value_pairs).astype(jnp.float32))
        return outputs.astype(jnp.bfloat16).reshape(per_step * stretch, heads_here * value_dim)
    mixed = lax.map(block_step, jnp.arange(blocks // per_step, dtype=jnp.int32))
    return mixed.reshape(frame_count, heads_here * value_dim)

def conv_silu(frames_rep, seg_row, w_dw):
    count = frames_rep.shape[0]
    half = KER // 2
    padded = jnp.pad(frames_rep.astype(jnp.float32), ((half, half), (0, 0)))
    seg_padded = jnp.pad(seg_row, (half, half), constant_values=-1)
    total = jnp.zeros(frames_rep.shape, jnp.float32)
    for offset in range(KER):
        same_rec = (seg_padded[offset:offset + count] == seg_row).astype(jnp.float32)
        total = total + w_dw[offset] * padded[offset:offset + count] * same_rec[:, None]
    return jax.nn.silu(total).astype(jnp.bfloat16)

def replica_forward(frames_rep, seg_row, look_row, w_dw, w_qkv, w_o):
    activ = conv_silu(frames_rep, seg_row, w_dw)
    qkv = jnp.dot(activ, w_qkv, preferred_element_type=jnp.float32).astype(jnp.bfloat16)

    def head_step(head):
        first = (head * HDIM).astype(jnp.int32)
        queries = lax.dynamic_slice_in_dim(qkv, first, HDIM, 1)
        keys = lax.dynamic_slice_in_dim(qkv, first + D, HDIM, 1)
        values = lax.dynamic_slice_in_dim(qkv, first + 2 * D, HDIM, 1)
        return stretch_attention(queries[:, None, :], keys[:, None, :], values[:, None, :], seg_row, look_row, STRETCH)
    per_head = lax.map(head_step, jnp.arange(HEADS, dtype=jnp.int32))
    attn = per_head.transpose(1, 0, 2).reshape(FR, D)
    mixed = jnp.dot(attn, w_o, preferred_element_type=jnp.float32).astype(jnp.bfloat16)
    return (mixed, attn)

def reference(frames, seg, look_back, w_dw, w_qkv, w_o, cotangent):
    stacked = frames.reshape(N_DP, FR, D)

    def replica_step(items):
        return replica_forward(items[0], items[1], items[2], w_dw, w_qkv, w_o)
    mixed, attn = lax.map(replica_step, (stacked, seg, look_back))
    mixed = mixed.reshape(FRAMES, D)
    weight_grad = lax.dot_general(attn.reshape(FRAMES, D).astype(jnp.float32), cotangent.astype(jnp.float32), (((0,), (0,)), ((), ())))
    return (mixed, weight_grad)
```

```python
import math

import jax
import jax.numpy as jnp
from jax import lax
from jax.sharding import PartitionSpec as P

KER = 5
HEADS = 16
HALF = KER // 2


def conv_silu(rows_in, seg_in, w_dw):
    count = rows_in.shape[0] - 2 * HALF
    own = seg_in[HALF : HALF + count]
    total = jnp.zeros((count, rows_in.shape[1]), jnp.float32)
    for offset in range(KER):
        same = (seg_in[offset : offset + count] == own).astype(jnp.float32)
        total = total + w_dw[offset] * rows_in[offset : offset + count].astype(jnp.float32) * same[:, None]
    return jax.nn.silu(total).astype(jnp.bfloat16)


def local(frames, seg, look_back, w_dw, w_qkv, w_o, cotangent):
    rows, width = frames.shape
    count = lax.axis_size("tm")
    me = lax.axis_index("tm")
    weights = lax.all_gather(w_qkv, "dp", axis=1, tiled=True)
    before = lax.ppermute(frames, "tm", [(i, i + 1) for i in range(count - 1)])
    far = lax.ppermute(frames[-HALF:], "tm", [(i, i + 2) for i in range(count - 2)])
    after = lax.ppermute(frames[:HALF], "tm", [(i + 1, i) for i in range(count - 1)])
    stack = jnp.concatenate([far, before, frames, after], 0)
    seg_padded = jnp.pad(seg[0], (rows + HALF, HALF), constant_values=-1)
    local_seg = lax.dynamic_slice_in_dim(seg_padded, me * rows, 2 * rows + 2 * HALF, 0)
    activ = conv_silu(stack, local_seg, w_dw)
    qkv = jnp.dot(activ[rows:], weights, preferred_element_type=jnp.float32).astype(jnp.bfloat16)
    kv_before = jnp.dot(
        activ[:rows], weights[:, width:], preferred_element_type=jnp.float32
    ).astype(jnp.bfloat16)
    head_dim = width // HEADS
    queries = qkv[:, :width].reshape(rows, HEADS, head_dim)
    kv = jnp.concatenate([kv_before, qkv[:, width:]], 0).reshape(2 * rows, 2, HEADS, head_dim)
    scores = jnp.einsum(
        "qhd,khd->hqk", queries, kv[:, 0], preferred_element_type=jnp.float32
    ) * (1.0 / math.sqrt(head_dim))
    seg_pair = local_seg[HALF : HALF + 2 * rows]
    same_rec = seg_pair[rows:][:, None] == seg_pair[None, :]
    look = lax.dynamic_slice_in_dim(look_back[0], me, 1, 0)[0] == 1
    allowed = same_rec & ((jnp.arange(2 * rows) >= rows) | look)[None, :]
    scores = jnp.where(allowed[None], scores, -1e30)
    raw = jnp.exp(scores - jnp.max(scores, axis=-1, keepdims=True))
    probs = (raw / jnp.sum(raw, axis=-1, keepdims=True)).astype(jnp.bfloat16)
    attn = jnp.einsum("hqk,khv->qhv", probs, kv[:, 1], preferred_element_type=jnp.float32)
    attn = attn.astype(jnp.bfloat16).reshape(rows, width)
    mixed = jnp.dot(attn, w_o, preferred_element_type=jnp.float32).astype(jnp.bfloat16)
    grad_term = lax.dot_general(
        attn, cotangent, (((0,), (0,)), ((), ())), preferred_element_type=jnp.float32
    )
    col_share = lax.psum_scatter(grad_term, "dp", scatter_dimension=1, tiled=True)
    weight_grad = lax.psum_scatter(col_share, "tm", scatter_dimension=0, tiled=True)
    return (mixed, weight_grad)


def solution(mesh):
    placed = (
        P(("dp", "tm"), None),
        P("dp", None),
        P("dp", None),
        P(),
        P(None, "dp"),
        P(),
        P(("dp", "tm"), None),
    )
    return jax.shard_map(
        local,
        mesh=mesh,
        in_specs=placed,
        out_specs=(P(("dp", "tm"), None), P("tm", "dp")),
        check_vma=False,
    )
```

```python
import functools
import math

import jax
import jax.numpy as jnp
from jax import lax
from jax.experimental import pallas as pl
from jax.experimental.pallas import tpu as pltpu
from jax.sharding import PartitionSpec as P

MESH = pl.DeviceIdType.MESH
BF = jnp.bfloat16
F32 = jnp.float32

KER = 5
HALF = 2
ROWS = 256
WIDTH = 1536
HDIM = 96
UNIT = 192
QUARTER = 48
PAIRS = 4
NX, NY, NZ = 4, 4, 8
COLS = 384
EDGE = 16
CHUNK = 64
NT = (((1,), (1,)), ((), ()))
DIRECT = 1


def dot(a, b):
    return jnp.dot(a, b, preferred_element_type=F32)


def dot_nt(a, b):
    return lax.dot_general(a, b, NT, preferred_element_type=F32)


def wait_for(ref, sem):
    pltpu.make_async_copy(ref, ref, sem).wait()


def identity(n):
    return (
        lax.broadcasted_iota(jnp.int32, (n, n), 0) == lax.broadcasted_iota(jnp.int32, (n, n), 1)
    ).astype(BF)


def kernel(
    frames, cmask, lohi, w_dw, w_qkv, cot, w_o, mixed, wgrad,
    wt, units, ext, halo, mask_b, acts, lohi_b, w_o_v, cot_sib, q_t, k_n, v_t, at, at_sib,
    gf, gb, r1, s1f, s1b, r2, s2b, r3,
    w_send, w_recv, f_send, halo_send, halo_recv, act_send, act_recv, small_send, small_recv,
    at_send, at_recv, g1_send, g1_recv, g2_send, g2_recv, g3_send, g3_recv, wo_sem,
):
    dp, tm = lax.axis_index("dp"), lax.axis_index("tm")
    y, c = lax.div(dp, 2), lax.rem(dp, 2)
    z, x = lax.div(tm, 4), lax.rem(tm, 4)
    oc = 1 - c

    def dev(yy, cc, zz, xx):
        return {"dp": yy * 2 + cc, "tm": zz * 4 + xx}

    def plus(v, d, n):
        return lax.rem(v + d, n)

    def rcopy(src, dst, send, recv, device):
        return pltpu.make_async_remote_copy(
            src_ref=src, dst_ref=dst, send_sem=send, recv_sem=recv,
            device_id=device, device_id_type=MESH,
        )

    sibling = dev(y, oc, z, x)
    following = {"dp": dp, "tm": plus(tm, 1, 32)}
    preceding = {"dp": dp, "tm": plus(tm, 31, 32)}
    x_low = dev(y, c, z, plus(x, NX - 1, NX))

    partners = [sibling, following, preceding]
    for d in range(1, NY):
        partners += [dev(plus(y, d, NY), c, z, x), dev(plus(y, d, NY), oc, z, x)]
    for d in range(1, NX):
        partners += [dev(y, c, z, plus(x, d, NX))]
    for d in range(1, NZ):
        partners += [dev(y, c, plus(z, d, NZ), x), dev(y, oc, plus(z, d, NZ), x)]
    barrier = pltpu.get_barrier_semaphore()
    for device in partners:
        pl.semaphore_signal(barrier, inc=1, device_id=device, device_id_type=MESH)

    wo_copy = pltpu.make_async_copy(w_o, w_o_v, wo_sem)
    wo_copy.start()
    eye = identity(3 * UNIT)

    def turn(i, _):
        part = pl.ds(pl.multiple_of(i * 256, 256), 256)
        turned = dot_nt(eye, w_qkv[part, :]).astype(BF)
        for j in range(3):
            wt[j, :, part] = turned[j * UNIT : (j + 1) * UNIT]
        return 0

    lax.fori_loop(0, WIDTH // 256, turn, 0)
    for o in range(KER):
        mask_b[o] = jnp.broadcast_to(cmask[:, o : o + 1], (ROWS, 128))
    ext[EDGE : EDGE + ROWS] = frames[...].astype(F32)
    lohi_b[c] = lohi[...]

    pl.semaphore_wait(barrier, len(partners))

    up = rcopy(frames.at[ROWS - EDGE : ROWS], halo.at[0], halo_send.at[0], halo_recv.at[0], following)
    down = rcopy(frames.at[0:EDGE], halo.at[1], halo_send.at[1], halo_recv.at[1], preceding)
    up.start()
    down.start()
    lohi_copy = rcopy(lohi, lohi_b.at[c], small_send.at[0], small_recv.at[0], sibling)
    lohi_copy.start()

    mine = lax.rem(x, 2) + 2 * lax.rem(z, 2)
    from_x = (1 - lax.rem(x, 2)) + 2 * lax.rem(z, 2)
    from_z = lax.rem(x, 2) + 2 * (1 - lax.rem(z, 2))
    from_xz = (1 - lax.rem(x, 2)) + 2 * (1 - lax.rem(z, 2))
    first = lax.rem(3 * dp, 4)
    offset = jnp.where(first == 3, 1, jnp.where(first == 2, 2, 0))

    def owned(jj):
        j = lax.rem(jj + offset, 3)
        u = 3 * dp + j
        return j, lax.rem(u, 4) * 3 + lax.div(u, 8), lax.rem(lax.div(u, 4), 2)

    def to_y(jj, d, e):
        j, idx, core = owned(jj)
        part = lax.rem(mine + e, 4)
        return rcopy(
            wt.at[j, pl.ds(pl.multiple_of(part * QUARTER, QUARTER), QUARTER)],
            units.at[idx, part], w_send.at[jj, d, e], w_recv.at[idx, part],
            dev(plus(y, d, NY), core, z, x),
        )

    def to_sibling(jj, e):
        j, idx, core = owned(jj)
        return rcopy(
            wt.at[j, e * QUARTER : (e + 1) * QUARTER],
            units.at[idx, e], w_send.at[jj, 0, e], w_recv.at[idx, e], sibling,
        )

    def send_own(jj, _):
        j, idx, core = owned(jj)
        for d in (1, 3, 2):
            to_y(jj, d, 0).start()

        @pl.when(idx < DIRECT)
        def _():
            for e in range(1, 4):
                for d in (1, 3, 2):
                    to_y(jj, d, e).start()

        @pl.when(core != c)
        def _():
            for e in range(4):
                to_sibling(jj, e).start()

        @pl.when(core == c)
        def _():
            for e in range(4):
                pltpu.make_async_copy(
                    wt.at[j, e * QUARTER : (e + 1) * QUARTER], units.at[idx, e], w_recv.at[idx, e]
                ).start()

        return 0

    lax.fori_loop(0, 3, send_own, 0)

    wait_for(halo.at[0], halo_recv.at[0])
    wait_for(halo.at[1], halo_recv.at[1])
    ext[0:EDGE] = halo[0].astype(F32)
    ext[EDGE + ROWS :] = halo[1].astype(F32)

    def act_copy(i, r):
        rows = pl.ds(r * CHUNK, CHUNK)
        device, place = ((sibling, 2 * c + 1), (following, 2 * c))[i]
        return rcopy(
            acts.at[2 * c + 1, rows], acts.at[place, rows], act_send.at[i, r], act_recv.at[i, r], device
        )

    def act_pass(r):
        rows = pl.ds(r * CHUNK, CHUNK)
        return rcopy(
            acts.at[2 * c, rows], acts.at[2 * c, rows], act_send.at[2, r], act_recv.at[2, r], sibling
        )

    for r in range(ROWS // CHUNK):

        def column(i, _, r=r):
            lanes = pl.ds(pl.multiple_of(i * 128, 128), 128)
            total = jnp.zeros((CHUNK, 128), F32)
            for o in range(KER):
                window = ext[EDGE - HALF + r * CHUNK + o : EDGE - HALF + r * CHUNK + o + CHUNK, lanes]
                total = total + w_dw[o : o + 1, lanes] * window * mask_b[o, r * CHUNK : (r + 1) * CHUNK]
            acts[2 * c + 1, r * CHUNK : (r + 1) * CHUNK, lanes] = (total / (1.0 + jnp.exp(-total))).astype(BF)
            return 0

        lax.fori_loop(0, WIDTH // 128, column, 0)
        act_copy(1, r).start()
        act_copy(0, r).start()

    cot_copy = rcopy(cot, cot_sib, small_send.at[1], small_recv.at[1], sibling)
    cot_copy.start()

    def foreign(hp, t):
        u = 8 * t + 4 * c + hp
        idx = hp * 3 + t
        return idx, (lax.div(u, 6) != y) & (idx >= DIRECT)

    def along_z(idx):
        step = jnp.where(lax.rem(idx, 2) == 0, 1, NZ - 1)
        return dev(y, c, plus(z, step, NZ), x)

    def pass_copy(idx, i):
        part = (mine, mine, from_x)[i]
        device = (x_low, along_z(idx), along_z(idx))[i]
        return rcopy(units.at[idx, part], units.at[idx, part], f_send.at[idx, i], w_recv.at[idx, part], device)

    def pump_first(hp):
        for t in range(3):
            idx, need = foreign(hp, t)

            @pl.when(need)
            def _(idx=idx):
                wait_for(units.at[idx, mine], w_recv.at[idx, mine])
                pass_copy(idx, 0).start()
                pass_copy(idx, 1).start()

    def pump_second(hp):
        for t in range(3):
            idx, need = foreign(hp, t)

            @pl.when(need)
            def _(idx=idx):
                wait_for(units.at[idx, from_x], w_recv.at[idx, from_x])
                pass_copy(idx, 2).start()

    def wait_unit(hp, t):
        idx, need = foreign(hp, t)

        @pl.when(need)
        def _():
            wait_for(units.at[idx, from_z], w_recv.at[idx, from_z])
            wait_for(units.at[idx, from_xz], w_recv.at[idx, from_xz])

        @pl.when(jnp.logical_not(need))
        def _():
            for e in range(4):
                wait_for(units.at[idx, e], w_recv.at[idx, e])

    def unit(hp, t):
        return units[hp * 3 + t].reshape(UNIT, WIDTH)

    def keys_values(hp, part):
        where = slice(part * ROWS, (part + 1) * ROWS)
        for s in range(2):
            k_n[hp, s, where] = dot_nt(acts[2 * s + part], unit(hp, 1)).astype(BF)
            v_t[hp, s, :, where] = dot_nt(unit(hp, 2), acts[2 * s + part]).astype(BF)

    def own_part(hp):
        for t in range(3):
            wait_unit(hp, t)
        for s in range(2):
            q_t[hp, s] = dot_nt(unit(hp, 0), acts[2 * s + 1]).astype(BF)
        keys_values(hp, 1)

    def advance(g, _):
        pl.when(g < PAIRS)(lambda: pump_first(g))
        pl.when((g >= 1) & (g <= PAIRS))(lambda: pump_second(g - 1))

        @pl.when(g == 2)
        def _():
            for r in range(ROWS // CHUNK):
                rows = pl.ds(r * CHUNK, CHUNK)
                wait_for(acts.at[2 * oc + 1, rows], act_recv.at[0, r])

        pl.when(g >= 2)(lambda: own_part(g - 2))

        @pl.when(g == PAIRS)
        def _():
            for r in range(ROWS // CHUNK):
                rows = pl.ds(r * CHUNK, CHUNK)
                wait_for(acts.at[2 * c, rows], act_recv.at[1, r])
                act_pass(r).start()

        return 0

    lax.fori_loop(0, PAIRS + 2, advance, 0)

    for r in range(ROWS // CHUNK):
        rows = pl.ds(r * CHUNK, CHUNK)
        wait_for(acts.at[2 * oc, rows], act_recv.at[2, r])
    wait_for(lohi_b.at[oc], small_recv.at[0])
    wait_for(cot_sib, small_recv.at[1])

    factor = math.log2(math.e) / math.sqrt(HDIM)

    def attend(hp):
        def one(s, _):
            q = q_t[hp, s]
            zero = jnp.zeros((HDIM, ROWS), BF)
            both = jnp.concatenate(
                [jnp.concatenate([q[:HDIM], zero], 0), jnp.concatenate([zero, q[HDIM:]], 0)], 1
            )
            scores = dot(k_n[hp, s], both)
            bounds = lohi_b[s]
            at_j = lax.broadcasted_iota(jnp.int32, (2 * ROWS, ROWS), 0)
            allowed = (at_j >= bounds[0:1]) & (at_j < bounds[1:2])
            for e in range(2):
                mine_scores = jnp.where(allowed, scores[:, e * ROWS : (e + 1) * ROWS], -1e30)
                top = jnp.max(mine_scores, axis=0, keepdims=True)
                raw = jnp.exp2((mine_scores - top) * factor)
                probs = (raw * (1.0 / jnp.sum(raw, axis=0, keepdims=True))).astype(BF)
                at[hp, s, e * HDIM : (e + 1) * HDIM] = dot(
                    v_t[hp, s, e * HDIM : (e + 1) * HDIM], probs
                ).astype(BF)
            return 0

        lax.fori_loop(0, 2, one, 0)

    def at_copy(hp):
        return rcopy(at.at[hp, oc], at_sib.at[hp], at_send.at[hp], at_recv.at[hp], sibling)

    def grad(hp):
        for v in range(NY):
            lanes = slice(v * COLS, (v + 1) * COLS)
            term = dot(at[hp, c], cot[:, lanes]) + dot(at[hp, oc], cot_sib[:, lanes])
            term = term.reshape(NX, QUARTER, COLS)
            gf[hp, v] = term
            gb[hp, v] = term.astype(BF)

    def g1_copy(hp, y_first, d):
        if y_first:
            to = plus(y, d, NY)
            src, device = gb.at[hp, to], dev(to, c, z, x)
        else:
            to = plus(x, d, NX)
            src, device = gb.at[hp, :, to], dev(y, c, z, to)
        return rcopy(src, r1.at[hp, d - 1], g1_send.at[hp, d - 1], g1_recv.at[hp, d - 1], device)

    def g2_copy(hp, y_first, d):
        if y_first:
            to = plus(x, d, NX)
            device = dev(y, c, z, to)
        else:
            to = plus(y, d, NY)
            device = dev(to, c, z, x)
        return rcopy(s1b.at[hp, to], r2.at[hp, d - 1], g2_send.at[hp, d - 1], g2_recv.at[hp, d - 1], device)

    def g3_copy(hp, core):
        return rcopy(
            s2b.at[hp], r3.at[z], g3_send.at[hp, core], g3_recv.at[z], dev(y, core, 4 * c + hp, x)
        )

    def g3_local(hp):
        return pltpu.make_async_copy(s2b.at[hp], r3.at[z], g3_recv.at[z])

    def sum_first(hp, y_first):
        for d in range(3):
            wait_for(r1.at[hp, d], g1_recv.at[hp, d])
        total = gf[hp, y] if y_first else gf[hp, :, x]
        for d in range(3):
            total = total + r1[hp, d].astype(F32)
        s1f[hp] = total
        s1b[hp] = total.astype(BF)
        for d in range(1, 4):
            g2_copy(hp, y_first, d).start()

    def sum_second(hp, y_first):
        for d in range(3):
            wait_for(r2.at[hp, d], g2_recv.at[hp, d])
        total = s1f[hp, x] if y_first else s1f[hp, y]
        for d in range(3):
            total = total + r2[hp, d].astype(F32)
        s2b[hp] = total.astype(BF)
        for core in range(2):
            own = (4 * c + hp == z) & (c == core)
            pl.when(own)(lambda: g3_local(hp).start())
            pl.when(jnp.logical_not(own))(lambda: g3_copy(hp, core).start())

    def heads(i, _):
        for odd in range(2):
            hp = 2 * i + odd
            y_first = odd == 0
            keys_values(hp, 0)
            attend(hp)
            at_copy(hp).start()
            grad(hp)
            for d in range(1, 4):
                g1_copy(hp, y_first, d).start()
            pl.when(hp >= 1)(lambda: sum_first(hp - 1, not y_first))
            pl.when(hp >= 2)(lambda: sum_second(hp - 2, y_first))
        return 0

    lax.fori_loop(0, PAIRS // 2, heads, 0)

    wo_copy.wait()
    small_eye = identity(ROWS)

    def project(part):
        total = None
        for hp in range(PAIRS):
            if part == 0:
                rows, core = at[hp, c], c
            else:
                rows, core = at_sib[hp], oc
            turned = dot_nt(small_eye, rows).astype(BF)
            start = pl.multiple_of(core * (PAIRS * UNIT) + hp * UNIT, UNIT)
            term = dot(turned, w_o_v[pl.ds(start, UNIT), :])
            total = term if total is None else total + term
        return total

    ext[0:ROWS] = project(0)
    sum_first(PAIRS - 1, False)
    sum_second(PAIRS - 2, True)
    for hp in range(PAIRS):
        wait_for(at_sib.at[hp], at_recv.at[hp])
    mixed[...] = (ext[0:ROWS] + project(1)).astype(BF)
    sum_second(PAIRS - 1, False)

    for v in range(NZ):
        wait_for(r3.at[v], g3_recv.at[v])
    total = r3[0].astype(F32)
    for v in range(1, NZ):
        total = total + r3[v].astype(F32)
    wgrad[...] = jnp.where(c == 0, total[:, :UNIT], total[:, UNIT:])

    up.wait_send()
    down.wait_send()
    lohi_copy.wait_send()
    cot_copy.wait_send()

    def sent_own(jj, _):
        j, idx, core = owned(jj)
        for d in (1, 3, 2):
            to_y(jj, d, 0).wait_send()

        @pl.when(idx < DIRECT)
        def _():
            for e in range(1, 4):
                for d in (1, 3, 2):
                    to_y(jj, d, e).wait_send()

        @pl.when(core != c)
        def _():
            for e in range(4):
                to_sibling(jj, e).wait_send()

        return 0

    lax.fori_loop(0, 3, sent_own, 0)
    for r in range(ROWS // CHUNK):
        act_copy(0, r).wait_send()
        act_copy(1, r).wait_send()
        act_pass(r).wait_send()

    def sent_parts(hp, _):
        for t in range(3):
            idx, need = foreign(hp, t)

            @pl.when(need)
            def _(idx=idx):
                for i in range(3):
                    pass_copy(idx, i).wait_send()

        at_copy(hp).wait_send()
        return 0

    lax.fori_loop(0, PAIRS, sent_parts, 0)
    for hp in range(PAIRS):
        for d in range(1, 4):
            g1_copy(hp, hp % 2 == 0, d).wait_send()
            g2_copy(hp, hp % 2 == 0, d).wait_send()
        for core in range(2):
            own = (4 * c + hp == z) & (c == core)
            pl.when(jnp.logical_not(own))(lambda: g3_copy(hp, core).wait_send())


def local(frames, seg, look_back, w_dw, w_qkv, w_o, cotangent):
    me = lax.axis_index("tm")
    row = jnp.pad(seg[0], (ROWS, HALF), constant_values=-1)
    row = lax.dynamic_slice_in_dim(row, me * ROWS, 2 * ROWS + HALF, 0)
    own = row[ROWS : 2 * ROWS]
    same = [
        (row[ROWS - HALF + o : 2 * ROWS - HALF + o] == own).astype(F32) for o in range(KER)
    ]
    cmask = jnp.stack(same + [jnp.zeros_like(same[0])] * 3, 1)
    pair = row[: 2 * ROWS]
    look = lax.dynamic_slice_in_dim(look_back[0], me, 1, 0)
    low = jnp.sum((pair[:, None] < own[None, :]).astype(jnp.int32), 0)
    high = jnp.sum((pair[:, None] <= own[None, :]).astype(jnp.int32), 0)
    low = jnp.maximum(low, jnp.where(look == 1, 0, ROWS))
    lohi = jnp.stack([low, high] + [jnp.zeros_like(low)] * 6, 0)
    vmem, hbm = pl.BlockSpec(memory_space=pltpu.VMEM), pl.BlockSpec(memory_space=pl.ANY)
    dma = pltpu.SemaphoreType.DMA
    return pl.pallas_call(
        kernel,
        name="block",
        out_shape=(
            jax.ShapeDtypeStruct((ROWS, WIDTH), BF),
            jax.ShapeDtypeStruct((QUARTER, UNIT), F32),
        ),
        in_specs=[vmem, vmem, vmem, vmem, vmem, vmem, hbm],
        out_specs=(vmem, vmem),
        scratch_shapes=[
            pltpu.VMEM((3, UNIT, WIDTH), BF),
            pltpu.VMEM((3 * PAIRS, 4, QUARTER, WIDTH), BF),
            pltpu.VMEM((ROWS + 2 * EDGE, WIDTH), F32),
            pltpu.VMEM((2, EDGE, WIDTH), BF),
            pltpu.VMEM((KER, ROWS, 128), F32),
            pltpu.VMEM((4, ROWS, WIDTH), BF),
            pltpu.VMEM((2, 8, ROWS), jnp.int32),
            pltpu.VMEM((WIDTH, WIDTH), BF),
            pltpu.VMEM((ROWS, WIDTH), BF),
            pltpu.VMEM((PAIRS, 2, UNIT, ROWS), BF),
            pltpu.VMEM((PAIRS, 2, 2 * ROWS, UNIT), BF),
            pltpu.VMEM((PAIRS, 2, UNIT, 2 * ROWS), BF),
            pltpu.VMEM((PAIRS, 2, UNIT, ROWS), BF),
            pltpu.VMEM((PAIRS, UNIT, ROWS), BF),
            pltpu.VMEM((PAIRS, NY, NX, QUARTER, COLS), F32),
            pltpu.VMEM((PAIRS, NY, NX, QUARTER, COLS), BF),
            pltpu.VMEM((PAIRS, 3, 4, QUARTER, COLS), BF),
            pltpu.VMEM((PAIRS, 4, QUARTER, COLS), F32),
            pltpu.VMEM((PAIRS, 4, QUARTER, COLS), BF),
            pltpu.VMEM((PAIRS, 3, QUARTER, COLS), BF),
            pltpu.VMEM((PAIRS, QUARTER, COLS), BF),
            pltpu.VMEM((NZ, QUARTER, COLS), BF),
            dma((3, 4, 4)),
            dma((3 * PAIRS, 4)),
            dma((3 * PAIRS, 3)),
            dma((2,)),
            dma((2,)),
            dma((3, 4)),
            dma((3, 4)),
            dma((2,)),
            dma((2,)),
            dma((PAIRS,)),
            dma((PAIRS,)),
            dma((PAIRS, 3)),
            dma((PAIRS, 3)),
            dma((PAIRS, 3)),
            dma((PAIRS, 3)),
            dma((PAIRS, 2)),
            dma((NZ,)),
            dma,
        ],
        compiler_params=pltpu.CompilerParams(
            collective_id=0, has_side_effects=True, vmem_limit_bytes=58 * 2**20
        ),
        cost_estimate=pl.CostEstimate(flops=10**10, bytes_accessed=10**7, transcendentals=2 * 10**6),
    )(frames, cmask, lohi, w_dw, w_qkv, cotangent, w_o)


def solution(mesh):
    placed = (
        P(("dp", "tm"), None),
        P("dp", None),
        P("dp", None),
        P(),
        P(None, "dp"),
        P(),
        P(("dp", "tm"), None),
    )
    return jax.shard_map(
        local,
        mesh=mesh,
        in_specs=placed,
        out_specs=(P(("dp", "tm"), None), P("tm", "dp")),
        check_vma=False,
    )
```

```python
import functools
import math

import jax
import jax.numpy as jnp
from jax import lax
from jax.experimental import pallas as pl
from jax.experimental.pallas import tpu as pltpu
from jax.sharding import PartitionSpec as P

MESH = pl.DeviceIdType.MESH
BF = jnp.bfloat16
F32 = jnp.float32

KER = 5
HALF = 2
ROWS = 256
WIDTH = 1536
HDIM = 96
UNIT = 192
QUARTER = 48
PAIRS = 4
NX, NY, NZ = 4, 4, 8
COLS = 384
SPLIT = 256
BUSY = 3
EDGE = 16
CHUNK = 64
NT = (((1,), (1,)), ((), ()))


def dot(a, b):
    return jnp.dot(a, b, preferred_element_type=F32)


def dot_nt(a, b):
    return lax.dot_general(a, b, NT, preferred_element_type=F32)


def wait_for(ref, sem):
    pltpu.make_async_copy(ref, ref, sem).wait()


def identity(n):
    return (
        lax.broadcasted_iota(jnp.int32, (n, n), 0) == lax.broadcasted_iota(jnp.int32, (n, n), 1)
    ).astype(BF)


def kernel(
    frames, seg, look, w_dw, wt, cot, w_o, mixed, wgrad,
    units, ext, halo, seg_b, mask_b, acts, lohi_b, w_o_v, cot_sib, q_t, k_n, v_t, at, at_sib,
    gf_a, gf_b, gb_a, gb_b, r1_a, r1_b, s1f_a, s1f_b, s1b_a, s1b_b, r2_a, r2_b, s2b, r3,
    w_send, w_recv, f_send, halo_send, halo_recv, act_send, act_recv, small_send, small_recv,
    at_send, at_recv, g1_send, g1_recv, g2_send, g2_recv, g3_send, g3_recv, wo_sem,
):
    dp, tm = lax.axis_index("dp"), lax.axis_index("tm")
    y, c = lax.div(dp, 2), lax.rem(dp, 2)
    z, x = lax.div(tm, 4), lax.rem(tm, 4)
    oc = 1 - c

    def dev(yy, cc, zz, xx):
        return {"dp": yy * 2 + cc, "tm": zz * 4 + xx}

    def plus(v, d, n):
        return lax.rem(v + d, n)

    def rcopy(src, dst, send, recv, device):
        return pltpu.make_async_remote_copy(
            src_ref=src, dst_ref=dst, send_sem=send, recv_sem=recv,
            device_id=device, device_id_type=MESH,
        )

    sibling = dev(y, oc, z, x)
    following = {"dp": dp, "tm": plus(tm, 1, 32)}
    preceding = {"dp": dp, "tm": plus(tm, 31, 32)}
    x_low = dev(y, c, z, plus(x, NX - 1, NX))

    partners = [sibling, following, preceding]
    for d in range(1, NY):
        partners += [dev(plus(y, d, NY), c, z, x), dev(plus(y, d, NY), oc, z, x)]
    for d in range(1, NX):
        partners += [dev(y, c, z, plus(x, d, NX))]
    for d in range(1, NZ):
        partners += [dev(y, c, plus(z, d, NZ), x), dev(y, oc, plus(z, d, NZ), x)]
    barrier = pltpu.get_barrier_semaphore()
    for device in partners:
        pl.semaphore_signal(barrier, inc=1, device_id=device, device_id_type=MESH)

    wo_copy = pltpu.make_async_copy(w_o, w_o_v, wo_sem)
    wo_copy.start()

    def seg_of(stretch, there):
        inside = jnp.clip(stretch, 0, 31)
        row = seg[:, pl.ds(pl.multiple_of(inside * ROWS, ROWS), ROWS)]
        return jnp.where(there, row, -1)

    seg_rows = [seg_of(tm - 1, tm > 0), seg_of(tm, tm >= 0), seg_of(tm + 1, tm < 31)]
    seg_cols = [jnp.transpose(jnp.broadcast_to(row, (128, ROWS))) for row in seg_rows]
    seg_b[0:EDGE] = seg_cols[0][ROWS - EDGE :]
    seg_b[EDGE : EDGE + ROWS] = seg_cols[1]
    seg_b[EDGE + ROWS :] = seg_cols[2][:EDGE]
    for o in range(KER):
        same = seg_b[EDGE - HALF + o : EDGE - HALF + o + ROWS] == seg_cols[1]
        mask_b[o] = jnp.where(same, 1.0, 0.0)
    looks = jnp.sum(
        jnp.where(lax.broadcasted_iota(jnp.int32, (1, 32), 1) == tm, look[...], 0), axis=1, keepdims=True
    )
    pair = jnp.concatenate([seg_cols[0], seg_cols[1]], 0)
    pair = jnp.concatenate([pair, pair], 1)
    low = jnp.sum(jnp.where(pair < seg_rows[1], 1, 0), axis=0, keepdims=True)
    high = jnp.sum(jnp.where(pair <= seg_rows[1], 1, 0), axis=0, keepdims=True)
    low = jnp.maximum(low, jnp.where(looks == 1, 0, ROWS))
    lohi_b[c, 0:1] = low
    lohi_b[c, 1:2] = high
    ext[EDGE : EDGE + ROWS] = frames[...].astype(F32)

    pl.semaphore_wait(barrier, len(partners))

    up = rcopy(frames.at[ROWS - EDGE : ROWS], halo.at[0], halo_send.at[0], halo_recv.at[0], following)
    down = rcopy(frames.at[0:EDGE], halo.at[1], halo_send.at[1], halo_recv.at[1], preceding)
    up.start()
    down.start()
    lohi_copy = rcopy(lohi_b.at[c], lohi_b.at[c], small_send.at[0], small_recv.at[0], sibling)
    lohi_copy.start()

    mine = lax.rem(x, 2) + 2 * lax.rem(z, 2)
    from_x = (1 - lax.rem(x, 2)) + 2 * lax.rem(z, 2)
    from_z = lax.rem(x, 2) + 2 * (1 - lax.rem(z, 2))
    from_xz = (1 - lax.rem(x, 2)) + 2 * (1 - lax.rem(z, 2))

    def owned(j):
        u = 3 * dp + j
        return lax.rem(u, 4), lax.div(u, 8), lax.rem(lax.div(u, 4), 2)

    def to_y(j, d):
        hp, t, core = owned(j)
        idx = hp * 3 + t
        return rcopy(
            wt.at[pl.ds(pl.multiple_of(j * UNIT + mine * QUARTER, QUARTER), QUARTER)],
            units.at[idx, mine], w_send.at[j, d], w_recv.at[idx, mine], dev(plus(y, d, NY), core, z, x),
        )

    def to_sibling(j, e):
        hp, t, core = owned(j)
        idx = hp * 3 + t
        return rcopy(
            wt.at[j * UNIT + e * QUARTER : j * UNIT + (e + 1) * QUARTER],
            units.at[idx, e], w_send.at[j, 4 + e], w_recv.at[idx, e], sibling,
        )

    def send_own(g):
        for j in range(3):
            hp, t, core = owned(j)
            idx = hp * 3 + t

            @pl.when(hp == g)
            def _(j=j):
                for d in (2, 1, 3):
                    to_y(j, d).start()

            @pl.when((hp == g) & (core != c))
            def _(j=j):
                for e in range(4):
                    to_sibling(j, e).start()

            @pl.when((hp == g) & (core == c))
            def _(j=j, idx=idx):
                for e in range(4):
                    pltpu.make_async_copy(
                        wt.at[j * UNIT + e * QUARTER : j * UNIT + (e + 1) * QUARTER],
                        units.at[idx, e], w_recv.at[idx, e],
                    ).start()

    send_own(0)
    send_own(1)

    wait_for(halo.at[0], halo_recv.at[0])
    wait_for(halo.at[1], halo_recv.at[1])
    ext[0:EDGE] = halo[0].astype(F32)
    ext[EDGE + ROWS :] = halo[1].astype(F32)

    def act_copy(i, r):
        rows = pl.ds(r * CHUNK, CHUNK)
        device, place = ((sibling, 2 * c + 1), (following, 2 * c))[i]
        return rcopy(
            acts.at[2 * c + 1, rows], acts.at[place, rows], act_send.at[i, r], act_recv.at[i, r], device
        )

    def act_pass(r):
        rows = pl.ds(r * CHUNK, CHUNK)
        return rcopy(
            acts.at[2 * c, rows], acts.at[2 * c, rows], act_send.at[2, r], act_recv.at[2, r], sibling
        )

    for r in range(ROWS // CHUNK):

        def column(i, _, r=r):
            lanes = pl.ds(pl.multiple_of(i * 128, 128), 128)
            total = jnp.zeros((CHUNK, 128), F32)
            for o in range(KER):
                window = ext[EDGE - HALF + r * CHUNK + o : EDGE - HALF + r * CHUNK + o + CHUNK, lanes]
                total = total + w_dw[o : o + 1, lanes] * window * mask_b[o, r * CHUNK : (r + 1) * CHUNK]
            acts[2 * c + 1, r * CHUNK : (r + 1) * CHUNK, lanes] = (total / (1.0 + jnp.exp(-total))).astype(BF)
            return 0

        lax.fori_loop(0, WIDTH // 128, column, 0)
        act_copy(1, r).start()
        act_copy(0, r).start()

    cot_copy = rcopy(cot, cot_sib, small_send.at[1], small_recv.at[1], sibling)
    cot_copy.start()

    def foreign(hp, t):
        u = 8 * t + 4 * c + hp
        idx = hp * 3 + t
        return idx, lax.div(u, 6) != y

    def along_z(idx):
        even = lax.rem(idx, 2) == 0
        third = lax.rem(lax.div(idx, 3) + lax.rem(idx, 3), 3) == 0
        step = jnp.where(jnp.where(x == BUSY, third, even), 1, NZ - 1)
        return dev(y, c, plus(z, step, NZ), x)

    def pass_copy(idx, t, i):
        part = (mine, mine, from_z if t == 2 else from_x)[i]
        late = dev(y, c, z, plus(x, jnp.where(idx >= 6, 1, NX - 1), NX))
        if i == 0:
            device = late if t == 0 else x_low
        elif i == 2 and t == 2:
            device = late
        else:
            device = along_z(idx)
        return rcopy(units.at[idx, part], units.at[idx, part], f_send.at[idx, i], w_recv.at[idx, part], device)

    def pump_first(hp):
        for t in range(3):
            idx, need = foreign(hp, t)

            @pl.when(need)
            def _(idx=idx, t=t):
                wait_for(units.at[idx, mine], w_recv.at[idx, mine])
                pass_copy(idx, t, 0).start()
                pass_copy(idx, t, 1).start()

    def pump_second(hp):
        for t in range(3):
            idx, need = foreign(hp, t)

            @pl.when(need)
            def _(idx=idx, t=t):
                arrived = from_z if t == 2 else from_x
                wait_for(units.at[idx, arrived], w_recv.at[idx, arrived])
                pass_copy(idx, t, 2).start()

    def wait_unit(hp, t):
        idx, need = foreign(hp, t)

        @pl.when(need)
        def _():
            other = from_x if t == 2 else from_z
            wait_for(units.at[idx, other], w_recv.at[idx, other])
            wait_for(units.at[idx, from_xz], w_recv.at[idx, from_xz])

        @pl.when(jnp.logical_not(need))
        def _():
            for e in range(4):
                wait_for(units.at[idx, e], w_recv.at[idx, e])

    def unit(hp, t):
        return units[hp * 3 + t].reshape(UNIT, WIDTH)

    def keys_values(hp, part):
        where = slice(part * ROWS, (part + 1) * ROWS)
        for s in range(2):
            k_n[hp, s, where] = dot_nt(acts[2 * s + part], unit(hp, 1)).astype(BF)
            v_t[hp, s, :, where] = dot_nt(unit(hp, 2), acts[2 * s + part]).astype(BF)

    def own_part(hp):
        for t in range(3):
            wait_unit(hp, t)
        for s in range(2):
            q_t[hp, s] = dot_nt(unit(hp, 0), acts[2 * s + 1]).astype(BF)
        keys_values(hp, 1)

    factor = math.log2(math.e) / math.sqrt(HDIM)

    def attend(hp):
        def one(s, _):
            q = q_t[hp, s]
            zero = jnp.zeros((HDIM, ROWS), BF)
            both = jnp.concatenate(
                [jnp.concatenate([q[:HDIM], zero], 0), jnp.concatenate([zero, q[HDIM:]], 0)], 1
            )
            scores = dot(k_n[hp, s], both)
            bounds = lohi_b[s]
            at_j = lax.broadcasted_iota(jnp.int32, (2 * ROWS, ROWS), 0)
            allowed = (at_j >= bounds[0:1]) & (at_j < bounds[1:2])
            for e in range(2):
                mine_scores = jnp.where(allowed, scores[:, e * ROWS : (e + 1) * ROWS], -1e30)
                top = jnp.max(mine_scores, axis=0, keepdims=True)
                raw = jnp.exp2((mine_scores - top) * factor)
                probs = (raw * (1.0 / jnp.sum(raw, axis=0, keepdims=True))).astype(BF)
                at[hp, s, e * HDIM : (e + 1) * HDIM] = dot(
                    v_t[hp, s, e * HDIM : (e + 1) * HDIM], probs
                ).astype(BF)
            return 0

        lax.fori_loop(0, 2, one, 0)

    def at_copy(hp):
        return rcopy(at.at[hp, oc], at_sib.at[hp], at_send.at[hp], at_recv.at[hp], sibling)

    def grad(hp):
        for v in range(NY):
            lanes = slice(v * COLS, (v + 1) * COLS)
            term = dot(at[hp, c], cot[:, lanes]) + dot(at[hp, oc], cot_sib[:, lanes])
            term = term.reshape(NX, QUARTER, COLS)

            def keep(wide_y):
                for i, lanes in enumerate((slice(0, SPLIT), slice(SPLIT, COLS))):
                    part = term[:, :, lanes]
                    if wide_y == (i == 0):
                        (gf_a, gf_b)[i][hp, v] = part
                        (gb_a, gb_b)[i][hp, v] = part.astype(BF)
                    else:
                        (gf_a, gf_b)[i][hp, :, v] = part
                        (gb_a, gb_b)[i][hp, :, v] = part.astype(BF)

            pl.when(lax.rem(hp, 2) == 0)(lambda keep=keep: keep(True))
            pl.when(lax.rem(hp, 2) == 1)(lambda keep=keep: keep(False))

    def along_y(hp, i, stage):
        return lax.rem(hp + i + stage, 2) == 0

    def toward(on_y, d):
        ty, tx = plus(y, d, NY), plus(x, d, NX)
        device = {"dp": jnp.where(on_y, ty * 2 + c, dp), "tm": jnp.where(on_y, tm, z * 4 + tx)}
        return jnp.where(on_y, ty, tx), device

    def own_place(on_y):
        return jnp.where(on_y, y, x)

    def g1_copy(hp, i, d):
        to, device = toward(along_y(hp, i, 0), d)
        return rcopy(
            (gb_a, gb_b)[i].at[hp, to], (r1_a, r1_b)[i].at[hp, d - 1],
            g1_send.at[hp, i, d - 1], g1_recv.at[hp, i, d - 1], device,
        )

    def g2_copy(hp, i, d):
        to, device = toward(along_y(hp, i, 1), d)
        return rcopy(
            (s1b_a, s1b_b)[i].at[hp, to], (r2_a, r2_b)[i].at[hp, d - 1],
            g2_send.at[hp, i, d - 1], g2_recv.at[hp, i, d - 1], device,
        )

    def g3_copy(hp, core):
        return rcopy(
            s2b.at[hp], r3.at[z], g3_send.at[hp, core], g3_recv.at[z], dev(y, core, 4 * c + hp, x)
        )

    def g3_local(hp):
        return pltpu.make_async_copy(s2b.at[hp], r3.at[z], g3_recv.at[z])

    def send_grad(hp):
        for d in (2, 1, 3):
            for i in range(2):
                g1_copy(hp, i, d).start()

    def sum_first(hp):
        for i in range(2):
            arrived, own = (r1_a, r1_b)[i], (gf_a, gf_b)[i]
            total = own[hp, own_place(along_y(hp, i, 0))]
            for d in (1, 3, 2):
                wait_for(arrived.at[hp, d - 1], g1_recv.at[hp, i, d - 1])
                total = total + arrived[hp, d - 1].astype(F32)
            (s1f_a, s1f_b)[i][hp] = total
            (s1b_a, s1b_b)[i][hp] = total.astype(BF)
            for d in (2, 1, 3):
                g2_copy(hp, i, d).start()

    def sum_second(hp):
        totals = []
        for i in range(2):
            arrived = (r2_a, r2_b)[i]
            total = (s1f_a, s1f_b)[i][hp, own_place(along_y(hp, i, 1))]
            for d in (1, 3, 2):
                wait_for(arrived.at[hp, d - 1], g2_recv.at[hp, i, d - 1])
                total = total + arrived[hp, d - 1].astype(F32)
            totals.append(total.astype(BF))
        s2b[hp] = jnp.concatenate(totals, 1)
        for core in range(2):
            own = (4 * c + hp == z) & (c == core)
            pl.when(own)(lambda: g3_local(hp).start())
            pl.when(jnp.logical_not(own))(lambda: g3_copy(hp, core).start())

    def chunks(act):
        for r in range(ROWS // CHUNK):
            act(r, pl.ds(r * CHUNK, CHUNK))

    def both_heads(hp):
        keys_values(hp, 0)
        attend(hp)
        at_copy(hp).start()
        grad(hp)
        send_grad(hp)

    def slot(g, _):
        pl.when(g < PAIRS - 1)(lambda: send_own(g + 1))
        pl.when(g < PAIRS + 1)(lambda: pump_first(g - 1))
        pl.when((g >= 2) & (g < PAIRS + 2))(lambda: pump_second(g - 2))

        @pl.when(g == 3)
        def _():
            chunks(lambda r, rows: wait_for(acts.at[2 * oc + 1, rows], act_recv.at[0, r]))

        pl.when((g >= 3) & (g <= 5))(lambda: own_part(g - 3))

        @pl.when(g == 4)
        def _():
            def onward(r, rows):
                wait_for(acts.at[2 * c, rows], act_recv.at[1, r])
                act_pass(r).start()

            chunks(onward)
            chunks(lambda r, rows: wait_for(acts.at[2 * oc, rows], act_recv.at[2, r]))
            wait_for(lohi_b.at[oc], small_recv.at[0])
            wait_for(cot_sib, small_recv.at[1])

        pl.when(g >= 4)(lambda: both_heads(g - 4))
        pl.when(g >= 6)(lambda: sum_first(g - 6))
        pl.when(g >= 7)(lambda: sum_second(g - 7))
        pl.when(g == 6)(lambda: own_part(PAIRS - 1))
        return 0

    lax.fori_loop(1, PAIRS + 4, slot, 0)

    wo_copy.wait()
    small_eye = identity(ROWS)

    def project(part):
        total = None
        for hp in range(PAIRS):
            if part == 0:
                rows, core = at[hp, c], c
            else:
                rows, core = at_sib[hp], oc
            turned = dot_nt(small_eye, rows).astype(BF)
            start = pl.multiple_of(core * (PAIRS * UNIT) + hp * UNIT, UNIT)
            term = dot(turned, w_o_v[pl.ds(start, UNIT), :])
            total = term if total is None else total + term
        return total

    ext[0:ROWS] = project(0)
    sum_first(PAIRS - 2)
    sum_second(PAIRS - 3)
    sum_first(PAIRS - 1)
    sum_second(PAIRS - 2)
    for hp in range(PAIRS):
        wait_for(at_sib.at[hp], at_recv.at[hp])
    mixed[...] = (ext[0:ROWS] + project(1)).astype(BF)
    sum_second(PAIRS - 1)

    for v in range(NZ):
        wait_for(r3.at[v], g3_recv.at[v])
    total = r3[0].astype(F32)
    for v in range(1, NZ):
        total = total + r3[v].astype(F32)
    wgrad[...] = jnp.where(c == 0, total[:, :UNIT], total[:, UNIT:])

    up.wait_send()
    down.wait_send()
    lohi_copy.wait_send()
    cot_copy.wait_send()

    for j in range(3):
        for d in (2, 1, 3):
            to_y(j, d).wait_send()

        @pl.when(owned(j)[2] != c)
        def _(j=j):
            for e in range(4):
                to_sibling(j, e).wait_send()

    for r in range(ROWS // CHUNK):
        act_copy(0, r).wait_send()
        act_copy(1, r).wait_send()
        act_pass(r).wait_send()

    def sent_parts(hp, _):
        for t in range(3):
            idx, need = foreign(hp, t)

            @pl.when(need)
            def _(idx=idx, t=t):
                for i in range(3):
                    pass_copy(idx, t, i).wait_send()

        at_copy(hp).wait_send()
        return 0

    lax.fori_loop(0, PAIRS, sent_parts, 0)
    for hp in range(PAIRS):
        for i in range(2):
            for d in range(1, 4):
                g1_copy(hp, i, d).wait_send()
                g2_copy(hp, i, d).wait_send()
        for core in range(2):
            own = (4 * c + hp == z) & (c == core)
            pl.when(jnp.logical_not(own))(lambda: g3_copy(hp, core).wait_send())


def local(frames, seg, look_back, w_dw, w_qkv, w_o, cotangent):
    vmem, hbm = pl.BlockSpec(memory_space=pltpu.VMEM), pl.BlockSpec(memory_space=pl.ANY)
    dma = pltpu.SemaphoreType.DMA
    return pl.pallas_call(
        kernel,
        name="block",
        out_shape=(
            jax.ShapeDtypeStruct((ROWS, WIDTH), BF),
            jax.ShapeDtypeStruct((QUARTER, UNIT), F32),
        ),
        in_specs=[vmem, vmem, vmem, vmem, vmem, vmem, hbm],
        out_specs=(vmem, vmem),
        scratch_shapes=[
            pltpu.VMEM((3 * PAIRS, 4, QUARTER, WIDTH), BF),
            pltpu.VMEM((ROWS + 2 * EDGE, WIDTH), F32),
            pltpu.VMEM((2, EDGE, WIDTH), BF),
            pltpu.VMEM((ROWS + 2 * EDGE, 128), jnp.int32),
            pltpu.VMEM((KER, ROWS, 128), F32),
            pltpu.VMEM((4, ROWS, WIDTH), BF),
            pltpu.VMEM((2, 8, ROWS), jnp.int32),
            pltpu.VMEM((WIDTH, WIDTH), BF),
            pltpu.VMEM((ROWS, WIDTH), BF),
            pltpu.VMEM((PAIRS, 2, UNIT, ROWS), BF),
            pltpu.VMEM((PAIRS, 2, 2 * ROWS, UNIT), BF),
            pltpu.VMEM((PAIRS, 2, UNIT, 2 * ROWS), BF),
            pltpu.VMEM((PAIRS, 2, UNIT, ROWS), BF),
            pltpu.VMEM((PAIRS, UNIT, ROWS), BF),
            pltpu.VMEM((PAIRS, 4, 4, QUARTER, SPLIT), F32),
            pltpu.VMEM((PAIRS, 4, 4, QUARTER, COLS - SPLIT), F32),
            pltpu.VMEM((PAIRS, 4, 4, QUARTER, SPLIT), BF),
            pltpu.VMEM((PAIRS, 4, 4, QUARTER, COLS - SPLIT), BF),
            pltpu.VMEM((PAIRS, 3, 4, QUARTER, SPLIT), BF),
            pltpu.VMEM((PAIRS, 3, 4, QUARTER, COLS - SPLIT), BF),
            pltpu.VMEM((PAIRS, 4, QUARTER, SPLIT), F32),
            pltpu.VMEM((PAIRS, 4, QUARTER, COLS - SPLIT), F32),
            pltpu.VMEM((PAIRS, 4, QUARTER, SPLIT), BF),
            pltpu.VMEM((PAIRS, 4, QUARTER, COLS - SPLIT), BF),
            pltpu.VMEM((PAIRS, 3, QUARTER, SPLIT), BF),
            pltpu.VMEM((PAIRS, 3, QUARTER, COLS - SPLIT), BF),
            pltpu.VMEM((PAIRS, QUARTER, COLS), BF),
            pltpu.VMEM((NZ, QUARTER, COLS), BF),
            dma((3, 8)),
            dma((3 * PAIRS, 4)),
            dma((3 * PAIRS, 3)),
            dma((2,)),
            dma((2,)),
            dma((3, 4)),
            dma((3, 4)),
            dma((2,)),
            dma((2,)),
            dma((PAIRS,)),
            dma((PAIRS,)),
            dma((PAIRS, 2, 3)),
            dma((PAIRS, 2, 3)),
            dma((PAIRS, 2, 3)),
            dma((PAIRS, 2, 3)),
            dma((PAIRS, 2)),
            dma((NZ,)),
            dma,
        ],
        compiler_params=pltpu.CompilerParams(
            collective_id=0, has_side_effects=True, vmem_limit_bytes=58 * 2**20
        ),
        cost_estimate=pl.CostEstimate(flops=10**10, bytes_accessed=10**7, transcendentals=2 * 10**6),
    )(frames, seg, look_back, w_dw, w_qkv.T, cotangent, w_o)


def solution(mesh):
    placed = (
        P(("dp", "tm"), None),
        P("dp", None),
        P("dp", None),
        P(),
        P(None, "dp"),
        P(),
        P(("dp", "tm"), None),
    )
    return jax.shard_map(
        local,
        mesh=mesh,
        in_specs=placed,
        out_specs=(P(("dp", "tm"), None), P("tm", "dp")),
        check_vma=False,
    )
```

```python
import functools
import math

import jax
import jax.numpy as jnp
from jax import lax
from jax.experimental import pallas as pl
from jax.experimental.pallas import tpu as pltpu
from jax.sharding import PartitionSpec as P

MESH = pl.DeviceIdType.MESH
BF = jnp.bfloat16
F32 = jnp.float32

KER = 5
HALF = 2
ROWS = 256
WIDTH = 1536
HDIM = 96
UNIT = 192
QUARTER = 48
PAIRS = 4
NX, NY, NZ = 4, 4, 8
COLS = 384
SPLIT = 256
BUSY = 3
EDGE = 16
CHUNK = 64
NT = (((1,), (1,)), ((), ()))


def dot(a, b):
    return jnp.dot(a, b, preferred_element_type=F32)


def dot_nt(a, b):
    return lax.dot_general(a, b, NT, preferred_element_type=F32)


def wait_for(ref, sem):
    pltpu.make_async_copy(ref, ref, sem).wait()


def identity(n):
    return (
        lax.broadcasted_iota(jnp.int32, (n, n), 0) == lax.broadcasted_iota(jnp.int32, (n, n), 1)
    ).astype(BF)


def kernel(
    frames, seg, look, w_dw, wt, cot, w_o, mixed, wgrad,
    units, ext, halo, seg_b, mask_b, acts, lohi_b, w_o_v, cot_sib, q_t, k_n, v_t, at, at_sib,
    gf_a, gf_b, gb_a, gb_b, r1_a, r1_b, s1f_a, s1f_b, s1b_a, s1b_b, r2_a, r2_b, s2b, r3,
    w_send, w_recv, f_send, halo_send, halo_recv, act_send, act_recv, small_send, small_recv,
    at_send, at_recv, g1_send, g1_recv, g2_send, g2_recv, g3_send, g3_recv, wo_sem,
):
    dp, tm = lax.axis_index("dp"), lax.axis_index("tm")
    y, c = lax.div(dp, 2), lax.rem(dp, 2)
    z, x = lax.div(tm, 4), lax.rem(tm, 4)
    oc = 1 - c

    def dev(yy, cc, zz, xx):
        return {"dp": yy * 2 + cc, "tm": zz * 4 + xx}

    def plus(v, d, n):
        return lax.rem(v + d, n)

    def rcopy(src, dst, send, recv, device):
        return pltpu.make_async_remote_copy(
            src_ref=src, dst_ref=dst, send_sem=send, recv_sem=recv,
            device_id=device, device_id_type=MESH,
        )

    sibling = dev(y, oc, z, x)
    following = {"dp": dp, "tm": plus(tm, 1, 32)}
    preceding = {"dp": dp, "tm": plus(tm, 31, 32)}
    x_low = dev(y, c, z, plus(x, NX - 1, NX))

    partners = [sibling, following, preceding]
    for d in range(1, NY):
        partners += [dev(plus(y, d, NY), c, z, x), dev(plus(y, d, NY), oc, z, x)]
    for d in range(1, NX):
        partners += [dev(y, c, z, plus(x, d, NX))]
    for d in range(1, NZ):
        partners += [dev(y, c, plus(z, d, NZ), x), dev(y, oc, plus(z, d, NZ), x)]
    barrier = pltpu.get_barrier_semaphore()
    for device in partners:
        pl.semaphore_signal(barrier, inc=1, device_id=device, device_id_type=MESH)

    wo_copy = pltpu.make_async_copy(w_o, w_o_v, wo_sem)
    wo_copy.start()

    def seg_of(stretch, there):
        inside = jnp.clip(stretch, 0, 31)
        row = seg[:, pl.ds(pl.multiple_of(inside * ROWS, ROWS), ROWS)]
        return jnp.where(there, row, -1)

    seg_rows = [seg_of(tm - 1, tm > 0), seg_of(tm, tm >= 0), seg_of(tm + 1, tm < 31)]
    seg_cols = [jnp.transpose(jnp.broadcast_to(row, (128, ROWS))) for row in seg_rows]
    seg_b[0:EDGE] = seg_cols[0][ROWS - EDGE :]
    seg_b[EDGE : EDGE + ROWS] = seg_cols[1]
    seg_b[EDGE + ROWS :] = seg_cols[2][:EDGE]
    for o in range(KER):
        same = seg_b[EDGE - HALF + o : EDGE - HALF + o + ROWS] == seg_cols[1]
        mask_b[o] = jnp.where(same, 1.0, 0.0)
    looks = jnp.sum(
        jnp.where(lax.broadcasted_iota(jnp.int32, (1, 32), 1) == tm, look[...], 0), axis=1, keepdims=True
    )
    pair = jnp.concatenate([seg_cols[0], seg_cols[1]], 0)
    pair = jnp.concatenate([pair, pair], 1)
    low = jnp.sum(jnp.where(pair < seg_rows[1], 1, 0), axis=0, keepdims=True)
    high = jnp.sum(jnp.where(pair <= seg_rows[1], 1, 0), axis=0, keepdims=True)
    low = jnp.maximum(low, jnp.where(looks == 1, 0, ROWS))
    lohi_b[c, 0:1] = low
    lohi_b[c, 1:2] = high
    ext[EDGE : EDGE + ROWS] = frames[...].astype(F32)

    pl.semaphore_wait(barrier, len(partners))

    up = rcopy(frames.at[ROWS - EDGE : ROWS], halo.at[0], halo_send.at[0], halo_recv.at[0], following)
    down = rcopy(frames.at[0:EDGE], halo.at[1], halo_send.at[1], halo_recv.at[1], preceding)
    up.start()
    down.start()
    lohi_copy = rcopy(lohi_b.at[c], lohi_b.at[c], small_send.at[0], small_recv.at[0], sibling)
    lohi_copy.start()

    mine = lax.rem(x, 2) + 2 * lax.rem(z, 2)
    from_x = (1 - lax.rem(x, 2)) + 2 * lax.rem(z, 2)
    from_z = lax.rem(x, 2) + 2 * (1 - lax.rem(z, 2))
    from_xz = (1 - lax.rem(x, 2)) + 2 * (1 - lax.rem(z, 2))

    def owned(j):
        u = 3 * dp + j
        return lax.rem(u, 4), lax.div(u, 8), lax.rem(lax.div(u, 4), 2)

    def to_y(j, d):
        hp, t, core = owned(j)
        idx = hp * 3 + t
        return rcopy(
            wt.at[pl.ds(pl.multiple_of(j * UNIT + mine * QUARTER, QUARTER), QUARTER)],
            units.at[idx, mine], w_send.at[j, d], w_recv.at[idx, mine], dev(plus(y, d, NY), core, z, x),
        )

    def to_sibling(j, e):
        hp, t, core = owned(j)
        idx = hp * 3 + t
        return rcopy(
            wt.at[j * UNIT + e * QUARTER : j * UNIT + (e + 1) * QUARTER],
            units.at[idx, e], w_send.at[j, 4 + e], w_recv.at[idx, e], sibling,
        )

    def send_own(g):
        for j in range(3):
            hp, t, core = owned(j)
            idx = hp * 3 + t

            @pl.when(hp == g)
            def _(j=j):
                for d in (2, 1, 3):
                    to_y(j, d).start()

            @pl.when((hp == g) & (core != c))
            def _(j=j):
                for e in range(4):
                    to_sibling(j, e).start()

            @pl.when((hp == g) & (core == c))
            def _(j=j, idx=idx):
                for e in range(4):
                    pltpu.make_async_copy(
                        wt.at[j * UNIT + e * QUARTER : j * UNIT + (e + 1) * QUARTER],
                        units.at[idx, e], w_recv.at[idx, e],
                    ).start()

    send_own(0)
    send_own(1)

    wait_for(halo.at[0], halo_recv.at[0])
    wait_for(halo.at[1], halo_recv.at[1])
    ext[0:EDGE] = halo[0].astype(F32)
    ext[EDGE + ROWS :] = halo[1].astype(F32)

    def act_copy(i, r):
        rows = pl.ds(r * CHUNK, CHUNK)
        device, place = ((sibling, 2 * c + 1), (following, 2 * c))[i]
        return rcopy(
            acts.at[2 * c + 1, rows], acts.at[place, rows], act_send.at[i, r], act_recv.at[i, r], device
        )

    def act_pass(r):
        rows = pl.ds(r * CHUNK, CHUNK)
        return rcopy(
            acts.at[2 * c, rows], acts.at[2 * c, rows], act_send.at[2, r], act_recv.at[2, r], sibling
        )

    for r in range(ROWS // CHUNK):

        def column(i, _, r=r):
            lanes = pl.ds(pl.multiple_of(i * 128, 128), 128)
            total = jnp.zeros((CHUNK, 128), F32)
            for o in range(KER):
                window = ext[EDGE - HALF + r * CHUNK + o : EDGE - HALF + r * CHUNK + o + CHUNK, lanes]
                total = total + w_dw[o : o + 1, lanes] * window * mask_b[o, r * CHUNK : (r + 1) * CHUNK]
            acts[2 * c + 1, r * CHUNK : (r + 1) * CHUNK, lanes] = (total / (1.0 + jnp.exp(-total))).astype(BF)
            return 0

        lax.fori_loop(0, WIDTH // 128, column, 0)
        act_copy(1, r).start()
        act_copy(0, r).start()

    cot_copy = rcopy(cot, cot_sib, small_send.at[1], small_recv.at[1], sibling)
    cot_copy.start()

    def foreign(hp, t):
        u = 8 * t + 4 * c + hp
        idx = hp * 3 + t
        return idx, lax.div(u, 6) != y

    def along_z(idx):
        even = lax.rem(idx, 2) == 0
        third = lax.rem(lax.div(idx, 3) + lax.rem(idx, 3), 3) == 0
        step = jnp.where(jnp.where(x == BUSY, third, even), 1, NZ - 1)
        return dev(y, c, plus(z, step, NZ), x)

    def pass_copy(idx, t, i):
        part = (mine, mine, from_z if t == 2 else from_x)[i]
        late = dev(y, c, z, plus(x, jnp.where(idx >= 3, 1, NX - 1), NX))
        if i == 0:
            device = late if t == 0 else x_low
        elif i == 2 and t == 2:
            device = late
        else:
            device = along_z(idx)
        return rcopy(units.at[idx, part], units.at[idx, part], f_send.at[idx, i], w_recv.at[idx, part], device)

    def pump_first(hp):
        for t in range(3):
            idx, need = foreign(hp, t)

            @pl.when(need)
            def _(idx=idx, t=t):
                wait_for(units.at[idx, mine], w_recv.at[idx, mine])
                pass_copy(idx, t, 0).start()
                pass_copy(idx, t, 1).start()

    def pump_second(hp):
        for t in range(3):
            idx, need = foreign(hp, t)

            @pl.when(need)
            def _(idx=idx, t=t):
                arrived = from_z if t == 2 else from_x
                wait_for(units.at[idx, arrived], w_recv.at[idx, arrived])
                pass_copy(idx, t, 2).start()

    def wait_unit(hp, t):
        idx, need = foreign(hp, t)

        @pl.when(need)
        def _():
            other = from_x if t == 2 else from_z
            wait_for(units.at[idx, other], w_recv.at[idx, other])
            wait_for(units.at[idx, from_xz], w_recv.at[idx, from_xz])

        @pl.when(jnp.logical_not(need))
        def _():
            for e in range(4):
                wait_for(units.at[idx, e], w_recv.at[idx, e])

    def unit(hp, t):
        return units[hp * 3 + t].reshape(UNIT, WIDTH)

    def keys_values(hp, part):
        where = slice(part * ROWS, (part + 1) * ROWS)
        for s in range(2):
            k_n[hp, s, where] = dot_nt(acts[2 * s + part], unit(hp, 1)).astype(BF)
            v_t[hp, s, :, where] = dot_nt(unit(hp, 2), acts[2 * s + part]).astype(BF)

    def own_part(hp):
        for t in range(3):
            wait_unit(hp, t)
        for s in range(2):
            q_t[hp, s] = dot_nt(unit(hp, 0), acts[2 * s + 1]).astype(BF)
        keys_values(hp, 1)

    factor = math.log2(math.e) / math.sqrt(HDIM)

    def attend(hp):
        def one(s, _):
            q = q_t[hp, s]
            zero = jnp.zeros((HDIM, ROWS), BF)
            both = jnp.concatenate(
                [jnp.concatenate([q[:HDIM], zero], 0), jnp.concatenate([zero, q[HDIM:]], 0)], 1
            )
            scores = dot(k_n[hp, s], both)
            bounds = lohi_b[s]
            at_j = lax.broadcasted_iota(jnp.int32, (2 * ROWS, ROWS), 0)
            allowed = (at_j >= bounds[0:1]) & (at_j < bounds[1:2])
            for e in range(2):
                mine_scores = jnp.where(allowed, scores[:, e * ROWS : (e + 1) * ROWS], -1e30)
                top = jnp.max(mine_scores, axis=0, keepdims=True)
                raw = jnp.exp2((mine_scores - top) * factor)
                probs = (raw * (1.0 / jnp.sum(raw, axis=0, keepdims=True))).astype(BF)
                at[hp, s, e * HDIM : (e + 1) * HDIM] = dot(
                    v_t[hp, s, e * HDIM : (e + 1) * HDIM], probs
                ).astype(BF)
            return 0

        lax.fori_loop(0, 2, one, 0)

    def at_copy(hp):
        return rcopy(at.at[hp, oc], at_sib.at[hp], at_send.at[hp], at_recv.at[hp], sibling)

    def grad(hp):
        for v in range(NY):
            lanes = slice(v * COLS, (v + 1) * COLS)
            term = dot(at[hp, c], cot[:, lanes]) + dot(at[hp, oc], cot_sib[:, lanes])
            term = term.reshape(NX, QUARTER, COLS)

            def keep(wide_y):
                for i, lanes in enumerate((slice(0, SPLIT), slice(SPLIT, COLS))):
                    part = term[:, :, lanes]
                    if wide_y == (i == 0):
                        (gf_a, gf_b)[i][hp, v] = part
                        (gb_a, gb_b)[i][hp, v] = part.astype(BF)
                    else:
                        (gf_a, gf_b)[i][hp, :, v] = part
                        (gb_a, gb_b)[i][hp, :, v] = part.astype(BF)

            pl.when(lax.rem(hp, 2) == 0)(lambda keep=keep: keep(True))
            pl.when(lax.rem(hp, 2) == 1)(lambda keep=keep: keep(False))

    def along_y(hp, i, stage):
        return lax.rem(hp + i + stage, 2) == 0

    def toward(on_y, d):
        ty, tx = plus(y, d, NY), plus(x, d, NX)
        device = {"dp": jnp.where(on_y, ty * 2 + c, dp), "tm": jnp.where(on_y, tm, z * 4 + tx)}
        return jnp.where(on_y, ty, tx), device

    def own_place(on_y):
        return jnp.where(on_y, y, x)

    def g1_copy(hp, i, d):
        to, device = toward(along_y(hp, i, 0), d)
        return rcopy(
            (gb_a, gb_b)[i].at[hp, to], (r1_a, r1_b)[i].at[hp, d - 1],
            g1_send.at[hp, i, d - 1], g1_recv.at[hp, i, d - 1], device,
        )

    def g2_copy(hp, i, d):
        to, device = toward(along_y(hp, i, 1), d)
        return rcopy(
            (s1b_a, s1b_b)[i].at[hp, to], (r2_a, r2_b)[i].at[hp, d - 1],
            g2_send.at[hp, i, d - 1], g2_recv.at[hp, i, d - 1], device,
        )

    def g3_copy(hp, core):
        return rcopy(
            s2b.at[hp], r3.at[z], g3_send.at[hp, core], g3_recv.at[z], dev(y, core, 4 * c + hp, x)
        )

    def g3_local(hp):
        return pltpu.make_async_copy(s2b.at[hp], r3.at[z], g3_recv.at[z])

    def send_grad(hp):
        for d in (2, 1, 3):
            for i in range(2):
                g1_copy(hp, i, d).start()

    def sum_first(hp):
        for i in range(2):
            arrived, own = (r1_a, r1_b)[i], (gf_a, gf_b)[i]
            total = own[hp, own_place(along_y(hp, i, 0))]
            for d in (1, 3, 2):
                wait_for(arrived.at[hp, d - 1], g1_recv.at[hp, i, d - 1])
                total = total + arrived[hp, d - 1].astype(F32)
            (s1f_a, s1f_b)[i][hp] = total
            (s1b_a, s1b_b)[i][hp] = total.astype(BF)
            for d in (2, 1, 3):
                g2_copy(hp, i, d).start()

    def sum_second(hp):
        totals = []
        for i in range(2):
            arrived = (r2_a, r2_b)[i]
            total = (s1f_a, s1f_b)[i][hp, own_place(along_y(hp, i, 1))]
            for d in (1, 3, 2):
                wait_for(arrived.at[hp, d - 1], g2_recv.at[hp, i, d - 1])
                total = total + arrived[hp, d - 1].astype(F32)
            totals.append(total.astype(BF))
        s2b[hp] = jnp.concatenate(totals, 1)
        for core in range(2):
            own = (4 * c + hp == z) & (c == core)
            pl.when(own)(lambda: g3_local(hp).start())
            pl.when(jnp.logical_not(own))(lambda: g3_copy(hp, core).start())

    def chunks(act):
        for r in range(ROWS // CHUNK):
            act(r, pl.ds(r * CHUNK, CHUNK))

    def both_heads(hp):
        keys_values(hp, 0)
        attend(hp)
        at_copy(hp).start()
        grad(hp)
        send_grad(hp)

    def slot(g, _):
        pl.when(g < PAIRS - 1)(lambda: send_own(g + 1))
        pl.when(g < PAIRS + 1)(lambda: pump_first(g - 1))
        pl.when((g >= 2) & (g < PAIRS + 2))(lambda: pump_second(g - 2))

        @pl.when(g == 3)
        def _():
            chunks(lambda r, rows: wait_for(acts.at[2 * oc + 1, rows], act_recv.at[0, r]))

        pl.when((g >= 3) & (g <= 5))(lambda: own_part(g - 3))

        @pl.when(g == 4)
        def _():
            def onward(r, rows):
                wait_for(acts.at[2 * c, rows], act_recv.at[1, r])
                act_pass(r).start()

            chunks(onward)
            chunks(lambda r, rows: wait_for(acts.at[2 * oc, rows], act_recv.at[2, r]))
            wait_for(lohi_b.at[oc], small_recv.at[0])
            wait_for(cot_sib, small_recv.at[1])

        pl.when(g >= 4)(lambda: both_heads(g - 4))
        pl.when(g >= 6)(lambda: sum_first(g - 6))
        pl.when(g >= 7)(lambda: sum_second(g - 7))
        pl.when(g == 6)(lambda: own_part(PAIRS - 1))
        return 0

    lax.fori_loop(1, PAIRS + 4, slot, 0)

    wo_copy.wait()
    small_eye = identity(ROWS)

    def project(part):
        total = None
        for hp in range(PAIRS):
            if part == 0:
                rows, core = at[hp, c], c
            else:
                rows, core = at_sib[hp], oc
            turned = dot_nt(small_eye, rows).astype(BF)
            start = pl.multiple_of(core * (PAIRS * UNIT) + hp * UNIT, UNIT)
            term = dot(turned, w_o_v[pl.ds(start, UNIT), :])
            total = term if total is None else total + term
        return total

    ext[0:ROWS] = project(0)
    sum_first(PAIRS - 2)
    sum_second(PAIRS - 3)
    sum_first(PAIRS - 1)
    sum_second(PAIRS - 2)
    for hp in range(PAIRS):
        wait_for(at_sib.at[hp], at_recv.at[hp])
    mixed[...] = (ext[0:ROWS] + project(1)).astype(BF)
    sum_second(PAIRS - 1)

    for v in range(NZ):
        wait_for(r3.at[v], g3_recv.at[v])
    total = r3[0].astype(F32)
    for v in range(1, NZ):
        total = total + r3[v].astype(F32)
    wgrad[...] = jnp.where(c == 0, total[:, :UNIT], total[:, UNIT:])

    up.wait_send()
    down.wait_send()
    lohi_copy.wait_send()
    cot_copy.wait_send()

    for j in range(3):
        for d in (2, 1, 3):
            to_y(j, d).wait_send()

        @pl.when(owned(j)[2] != c)
        def _(j=j):
            for e in range(4):
                to_sibling(j, e).wait_send()

    for r in range(ROWS // CHUNK):
        act_copy(0, r).wait_send()
        act_copy(1, r).wait_send()
        act_pass(r).wait_send()

    def sent_parts(hp, _):
        for t in range(3):
            idx, need = foreign(hp, t)

            @pl.when(need)
            def _(idx=idx, t=t):
                for i in range(3):
                    pass_copy(idx, t, i).wait_send()

        at_copy(hp).wait_send()
        return 0

    lax.fori_loop(0, PAIRS, sent_parts, 0)
    for hp in range(PAIRS):
        for i in range(2):
            for d in range(1, 4):
                g1_copy(hp, i, d).wait_send()
                g2_copy(hp, i, d).wait_send()
        for core in range(2):
            own = (4 * c + hp == z) & (c == core)
            pl.when(jnp.logical_not(own))(lambda: g3_copy(hp, core).wait_send())


def local(frames, seg, look_back, w_dw, w_qkv, w_o, cotangent):
    vmem, hbm = pl.BlockSpec(memory_space=pltpu.VMEM), pl.BlockSpec(memory_space=pl.ANY)
    dma = pltpu.SemaphoreType.DMA
    return pl.pallas_call(
        kernel,
        name="block",
        out_shape=(
            jax.ShapeDtypeStruct((ROWS, WIDTH), BF),
            jax.ShapeDtypeStruct((QUARTER, UNIT), F32),
        ),
        in_specs=[vmem, vmem, vmem, vmem, vmem, vmem, hbm],
        out_specs=(vmem, vmem),
        scratch_shapes=[
            pltpu.VMEM((3 * PAIRS, 4, QUARTER, WIDTH), BF),
            pltpu.VMEM((ROWS + 2 * EDGE, WIDTH), F32),
            pltpu.VMEM((2, EDGE, WIDTH), BF),
            pltpu.VMEM((ROWS + 2 * EDGE, 128), jnp.int32),
            pltpu.VMEM((KER, ROWS, 128), F32),
            pltpu.VMEM((4, ROWS, WIDTH), BF),
            pltpu.VMEM((2, 8, ROWS), jnp.int32),
            pltpu.VMEM((WIDTH, WIDTH), BF),
            pltpu.VMEM((ROWS, WIDTH), BF),
            pltpu.VMEM((PAIRS, 2, UNIT, ROWS), BF),
            pltpu.VMEM((PAIRS, 2, 2 * ROWS, UNIT), BF),
            pltpu.VMEM((PAIRS, 2, UNIT, 2 * ROWS), BF),
            pltpu.VMEM((PAIRS, 2, UNIT, ROWS), BF),
            pltpu.VMEM((PAIRS, UNIT, ROWS), BF),
            pltpu.VMEM((PAIRS, 4, 4, QUARTER, SPLIT), F32),
            pltpu.VMEM((PAIRS, 4, 4, QUARTER, COLS - SPLIT), F32),
            pltpu.VMEM((PAIRS, 4, 4, QUARTER, SPLIT), BF),
            pltpu.VMEM((PAIRS, 4, 4, QUARTER, COLS - SPLIT), BF),
            pltpu.VMEM((PAIRS, 3, 4, QUARTER, SPLIT), BF),
            pltpu.VMEM((PAIRS, 3, 4, QUARTER, COLS - SPLIT), BF),
            pltpu.VMEM((PAIRS, 4, QUARTER, SPLIT), F32),
            pltpu.VMEM((PAIRS, 4, QUARTER, COLS - SPLIT), F32),
            pltpu.VMEM((PAIRS, 4, QUARTER, SPLIT), BF),
            pltpu.VMEM((PAIRS, 4, QUARTER, COLS - SPLIT), BF),
            pltpu.VMEM((PAIRS, 3, QUARTER, SPLIT), BF),
            pltpu.VMEM((PAIRS, 3, QUARTER, COLS - SPLIT), BF),
            pltpu.VMEM((PAIRS, QUARTER, COLS), BF),
            pltpu.VMEM((NZ, QUARTER, COLS), BF),
            dma((3, 8)),
            dma((3 * PAIRS, 4)),
            dma((3 * PAIRS, 3)),
            dma((2,)),
            dma((2,)),
            dma((3, 4)),
            dma((3, 4)),
            dma((2,)),
            dma((2,)),
            dma((PAIRS,)),
            dma((PAIRS,)),
            dma((PAIRS, 2, 3)),
            dma((PAIRS, 2, 3)),
            dma((PAIRS, 2, 3)),
            dma((PAIRS, 2, 3)),
            dma((PAIRS, 2)),
            dma((NZ,)),
            dma,
        ],
        compiler_params=pltpu.CompilerParams(
            collective_id=0, has_side_effects=True, vmem_limit_bytes=58 * 2**20
        ),
        cost_estimate=pl.CostEstimate(flops=10**10, bytes_accessed=10**7, transcendentals=2 * 10**6),
    )(frames, seg, look_back, w_dw, w_qkv.T, cotangent, w_o)


def solution(mesh):
    placed = (
        P(("dp", "tm"), None),
        P("dp", None),
        P("dp", None),
        P(),
        P(None, "dp"),
        P(),
        P(("dp", "tm"), None),
    )
    return jax.shard_map(
        local,
        mesh=mesh,
        in_specs=placed,
        out_specs=(P(("dp", "tm"), None), P("tm", "dp")),
        check_vma=False,
    )
```

```python
import functools
import math

import jax
import jax.numpy as jnp
from jax import lax
from jax.experimental import pallas as pl
from jax.experimental.pallas import tpu as pltpu
from jax.sharding import PartitionSpec as P

MESH = pl.DeviceIdType.MESH
BF = jnp.bfloat16
F32 = jnp.float32

KER = 5
HALF = 2
ROWS = 256
WIDTH = 1536
HDIM = 96
UNIT = 192
QUARTER = 48
PAIRS = 4
NX, NY, NZ = 4, 4, 8
COLS = 384
SPLIT = 128
BUSY = 3
EDGE = 16
CHUNK = 64
NT = (((1,), (1,)), ((), ()))


def dot(a, b):
    return jnp.dot(a, b, preferred_element_type=F32)


def dot_nt(a, b):
    return lax.dot_general(a, b, NT, preferred_element_type=F32)


def wait_for(ref, sem):
    pltpu.make_async_copy(ref, ref, sem).wait()


def identity(n):
    return (
        lax.broadcasted_iota(jnp.int32, (n, n), 0) == lax.broadcasted_iota(jnp.int32, (n, n), 1)
    ).astype(BF)


def kernel(
    frames, seg, look, w_dw, wt, cot, w_o, mixed, wgrad,
    units, ext, halo, seg_b, mask_b, acts, lohi_b, w_o_v, cot_sib, q_t, k_n, v_t, at, at_sib,
    gf_a, gf_b, gb_a, gb_b, r1_a, r1_b, s1f_a, s1f_b, s1b_a, s1b_b, r2_a, r2_b, s2b, r3,
    w_send, w_recv, f_send, halo_send, halo_recv, act_send, act_recv, small_send, small_recv,
    at_send, at_recv, g1_send, g1_recv, g2_send, g2_recv, g3_send, g3_recv, wo_sem,
):
    dp, tm = lax.axis_index("dp"), lax.axis_index("tm")
    y, c = lax.div(dp, 2), lax.rem(dp, 2)
    z, x = lax.div(tm, 4), lax.rem(tm, 4)
    oc = 1 - c

    def dev(yy, cc, zz, xx):
        return {"dp": yy * 2 + cc, "tm": zz * 4 + xx}

    def plus(v, d, n):
        return lax.rem(v + d, n)

    def rcopy(src, dst, send, recv, device):
        return pltpu.make_async_remote_copy(
            src_ref=src, dst_ref=dst, send_sem=send, recv_sem=recv,
            device_id=device, device_id_type=MESH,
        )

    sibling = dev(y, oc, z, x)
    following = {"dp": dp, "tm": plus(tm, 1, 32)}
    preceding = {"dp": dp, "tm": plus(tm, 31, 32)}
    x_low = dev(y, c, z, plus(x, NX - 1, NX))

    partners = [sibling, following, preceding]
    for d in range(1, NY):
        partners += [dev(plus(y, d, NY), c, z, x), dev(plus(y, d, NY), oc, z, x)]
    for d in range(1, NX):
        partners += [dev(y, c, z, plus(x, d, NX))]
    for d in range(1, NZ):
        partners += [dev(y, c, plus(z, d, NZ), x), dev(y, oc, plus(z, d, NZ), x)]
    barrier = pltpu.get_barrier_semaphore()
    for device in partners:
        pl.semaphore_signal(barrier, inc=1, device_id=device, device_id_type=MESH)

    wo_copy = pltpu.make_async_copy(w_o, w_o_v, wo_sem)
    wo_copy.start()

    def seg_of(stretch, there):
        inside = jnp.clip(stretch, 0, 31)
        row = seg[:, pl.ds(pl.multiple_of(inside * ROWS, ROWS), ROWS)]
        return jnp.where(there, row, -1)

    seg_rows = [seg_of(tm - 1, tm > 0), seg_of(tm, tm >= 0), seg_of(tm + 1, tm < 31)]
    seg_cols = [jnp.transpose(jnp.broadcast_to(row, (128, ROWS))) for row in seg_rows]
    seg_b[0:EDGE] = seg_cols[0][ROWS - EDGE :]
    seg_b[EDGE : EDGE + ROWS] = seg_cols[1]
    seg_b[EDGE + ROWS :] = seg_cols[2][:EDGE]
    for o in range(KER):
        same = seg_b[EDGE - HALF + o : EDGE - HALF + o + ROWS] == seg_cols[1]
        mask_b[o] = jnp.where(same, 1.0, 0.0)
    looks = jnp.sum(
        jnp.where(lax.broadcasted_iota(jnp.int32, (1, 32), 1) == tm, look[...], 0), axis=1, keepdims=True
    )
    pair = jnp.concatenate([seg_cols[0], seg_cols[1]], 0)
    pair = jnp.concatenate([pair, pair], 1)
    low = jnp.sum(jnp.where(pair < seg_rows[1], 1, 0), axis=0, keepdims=True)
    high = jnp.sum(jnp.where(pair <= seg_rows[1], 1, 0), axis=0, keepdims=True)
    low = jnp.maximum(low, jnp.where(looks == 1, 0, ROWS))
    lohi_b[c, 0:1] = low
    lohi_b[c, 1:2] = high
    ext[EDGE : EDGE + ROWS] = frames[...].astype(F32)

    pl.semaphore_wait(barrier, len(partners))

    up = rcopy(frames.at[ROWS - EDGE : ROWS], halo.at[0], halo_send.at[0], halo_recv.at[0], following)
    down = rcopy(frames.at[0:EDGE], halo.at[1], halo_send.at[1], halo_recv.at[1], preceding)
    up.start()
    down.start()
    lohi_copy = rcopy(lohi_b.at[c], lohi_b.at[c], small_send.at[0], small_recv.at[0], sibling)
    lohi_copy.start()

    mine = lax.rem(x, 2) + 2 * lax.rem(z, 2)
    from_x = (1 - lax.rem(x, 2)) + 2 * lax.rem(z, 2)
    from_z = lax.rem(x, 2) + 2 * (1 - lax.rem(z, 2))
    from_xz = (1 - lax.rem(x, 2)) + 2 * (1 - lax.rem(z, 2))

    def owned(j):
        u = 3 * dp + j
        return lax.rem(u, 4), lax.div(u, 8), lax.rem(lax.div(u, 4), 2)

    def to_y(j, d):
        hp, t, core = owned(j)
        idx = hp * 3 + t
        return rcopy(
            wt.at[pl.ds(pl.multiple_of(j * UNIT + mine * QUARTER, QUARTER), QUARTER)],
            units.at[idx, mine], w_send.at[j, d], w_recv.at[idx, mine], dev(plus(y, d, NY), core, z, x),
        )

    def to_sibling(j, e):
        hp, t, core = owned(j)
        idx = hp * 3 + t
        return rcopy(
            wt.at[j * UNIT + e * QUARTER : j * UNIT + (e + 1) * QUARTER],
            units.at[idx, e], w_send.at[j, 4 + e], w_recv.at[idx, e], sibling,
        )

    def send_own(g):
        for j in range(3):
            hp, t, core = owned(j)
            idx = hp * 3 + t

            @pl.when(hp == g)
            def _(j=j):
                for d in (2, 1, 3):
                    to_y(j, d).start()

            @pl.when((hp == g) & (core != c))
            def _(j=j):
                for e in range(4):
                    to_sibling(j, e).start()

            @pl.when((hp == g) & (core == c))
            def _(j=j, idx=idx):
                for e in range(4):
                    pltpu.make_async_copy(
                        wt.at[j * UNIT + e * QUARTER : j * UNIT + (e + 1) * QUARTER],
                        units.at[idx, e], w_recv.at[idx, e],
                    ).start()

    send_own(0)
    send_own(1)

    wait_for(halo.at[0], halo_recv.at[0])
    wait_for(halo.at[1], halo_recv.at[1])
    ext[0:EDGE] = halo[0].astype(F32)
    ext[EDGE + ROWS :] = halo[1].astype(F32)

    def act_copy(i, r):
        rows = pl.ds(r * CHUNK, CHUNK)
        device, place = ((sibling, 2 * c + 1), (following, 2 * c))[i]
        return rcopy(
            acts.at[2 * c + 1, rows], acts.at[place, rows], act_send.at[i, r], act_recv.at[i, r], device
        )

    def act_pass(r):
        rows = pl.ds(r * CHUNK, CHUNK)
        return rcopy(
            acts.at[2 * c, rows], acts.at[2 * c, rows], act_send.at[2, r], act_recv.at[2, r], sibling
        )

    for r in range(ROWS // CHUNK):

        def column(i, _, r=r):
            lanes = pl.ds(pl.multiple_of(i * 128, 128), 128)
            total = jnp.zeros((CHUNK, 128), F32)
            for o in range(KER):
                window = ext[EDGE - HALF + r * CHUNK + o : EDGE - HALF + r * CHUNK + o + CHUNK, lanes]
                total = total + w_dw[o : o + 1, lanes] * window * mask_b[o, r * CHUNK : (r + 1) * CHUNK]
            acts[2 * c + 1, r * CHUNK : (r + 1) * CHUNK, lanes] = (total / (1.0 + jnp.exp(-total))).astype(BF)
            return 0

        lax.fori_loop(0, WIDTH // 128, column, 0)
        act_copy(1, r).start()
        act_copy(0, r).start()

    cot_copy = rcopy(cot, cot_sib, small_send.at[1], small_recv.at[1], sibling)
    cot_copy.start()

    def foreign(hp, t):
        u = 8 * t + 4 * c + hp
        idx = hp * 3 + t
        return idx, lax.div(u, 6) != y

    def along_z(idx):
        even = lax.rem(idx, 2) == 0
        third = lax.rem(lax.div(idx, 3) + lax.rem(idx, 3), 3) == 0
        step = jnp.where(jnp.where(x == BUSY, third, even), 1, NZ - 1)
        return dev(y, c, plus(z, step, NZ), x)

    def pass_copy(idx, t, i):
        part = (mine, mine, from_z if t == 2 else from_x)[i]
        late = dev(y, c, z, plus(x, jnp.where(idx >= 3, 1, NX - 1), NX))
        if i == 0:
            device = late if t == 0 else x_low
        elif i == 2 and t == 2:
            device = late
        else:
            device = along_z(idx)
        return rcopy(units.at[idx, part], units.at[idx, part], f_send.at[idx, i], w_recv.at[idx, part], device)

    def pump_first(hp):
        for t in range(3):
            idx, need = foreign(hp, t)

            @pl.when(need)
            def _(idx=idx, t=t):
                wait_for(units.at[idx, mine], w_recv.at[idx, mine])
                pass_copy(idx, t, 0).start()
                pass_copy(idx, t, 1).start()

    def pump_second(hp):
        for t in range(3):
            idx, need = foreign(hp, t)

            @pl.when(need)
            def _(idx=idx, t=t):
                arrived = from_z if t == 2 else from_x
                wait_for(units.at[idx, arrived], w_recv.at[idx, arrived])
                pass_copy(idx, t, 2).start()

    def wait_unit(hp, t):
        idx, need = foreign(hp, t)

        @pl.when(need)
        def _():
            other = from_x if t == 2 else from_z
            wait_for(units.at[idx, other], w_recv.at[idx, other])
            wait_for(units.at[idx, from_xz], w_recv.at[idx, from_xz])

        @pl.when(jnp.logical_not(need))
        def _():
            for e in range(4):
                wait_for(units.at[idx, e], w_recv.at[idx, e])

    def unit(hp, t):
        return units[hp * 3 + t].reshape(UNIT, WIDTH)

    def keys_values(hp, part):
        where = slice(part * ROWS, (part + 1) * ROWS)
        for s in range(2):
            k_n[hp, s, where] = dot_nt(acts[2 * s + part], unit(hp, 1)).astype(BF)
            v_t[hp, s, :, where] = dot_nt(unit(hp, 2), acts[2 * s + part]).astype(BF)

    def own_part(hp):
        for t in range(3):
            wait_unit(hp, t)
        for s in range(2):
            q_t[hp, s] = dot_nt(unit(hp, 0), acts[2 * s + 1]).astype(BF)
        keys_values(hp, 1)

    factor = math.log2(math.e) / math.sqrt(HDIM)

    def attend(hp):
        def one(s, _):
            q = q_t[hp, s]
            zero = jnp.zeros((HDIM, ROWS), BF)
            both = jnp.concatenate(
                [jnp.concatenate([q[:HDIM], zero], 0), jnp.concatenate([zero, q[HDIM:]], 0)], 1
            )
            scores = dot(k_n[hp, s], both)
            bounds = lohi_b[s]
            at_j = lax.broadcasted_iota(jnp.int32, (2 * ROWS, ROWS), 0)
            allowed = (at_j >= bounds[0:1]) & (at_j < bounds[1:2])
            for e in range(2):
                mine_scores = jnp.where(allowed, scores[:, e * ROWS : (e + 1) * ROWS], -1e30)
                top = jnp.max(mine_scores, axis=0, keepdims=True)
                raw = jnp.exp2((mine_scores - top) * factor)
                probs = (raw * (1.0 / jnp.sum(raw, axis=0, keepdims=True))).astype(BF)
                at[hp, s, e * HDIM : (e + 1) * HDIM] = dot(
                    v_t[hp, s, e * HDIM : (e + 1) * HDIM], probs
                ).astype(BF)
            return 0

        lax.fori_loop(0, 2, one, 0)

    def at_copy(hp):
        return rcopy(at.at[hp, oc], at_sib.at[hp], at_send.at[hp], at_recv.at[hp], sibling)

    def grad(hp):
        for v in range(NY):
            lanes = slice(v * COLS, (v + 1) * COLS)
            term = dot(at[hp, c], cot[:, lanes]) + dot(at[hp, oc], cot_sib[:, lanes])
            term = term.reshape(NX, QUARTER, COLS)

            def keep(wide_y):
                for i, lanes in enumerate((slice(0, SPLIT), slice(SPLIT, COLS))):
                    part = term[:, :, lanes]
                    if wide_y == (i == 0):
                        (gf_a, gf_b)[i][hp, v] = part
                        (gb_a, gb_b)[i][hp, v] = part.astype(BF)
                    else:
                        (gf_a, gf_b)[i][hp, :, v] = part
                        (gb_a, gb_b)[i][hp, :, v] = part.astype(BF)

            pl.when(lax.rem(hp, 2) == 0)(lambda keep=keep: keep(True))
            pl.when(lax.rem(hp, 2) == 1)(lambda keep=keep: keep(False))

    def along_y(hp, i, stage):
        return lax.rem(hp + i + stage, 2) == 0

    def toward(on_y, d):
        ty, tx = plus(y, d, NY), plus(x, d, NX)
        device = {"dp": jnp.where(on_y, ty * 2 + c, dp), "tm": jnp.where(on_y, tm, z * 4 + tx)}
        return jnp.where(on_y, ty, tx), device

    def own_place(on_y):
        return jnp.where(on_y, y, x)

    def g1_copy(hp, i, d):
        to, device = toward(along_y(hp, i, 0), d)
        return rcopy(
            (gb_a, gb_b)[i].at[hp, to], (r1_a, r1_b)[i].at[hp, d - 1],
            g1_send.at[hp, i, d - 1], g1_recv.at[hp, i, d - 1], device,
        )

    def g2_copy(hp, i, d):
        to, device = toward(along_y(hp, i, 1), d)
        return rcopy(
            (s1b_a, s1b_b)[i].at[hp, to], (r2_a, r2_b)[i].at[hp, d - 1],
            g2_send.at[hp, i, d - 1], g2_recv.at[hp, i, d - 1], device,
        )

    def g3_copy(hp, core):
        return rcopy(
            s2b.at[hp], r3.at[z], g3_send.at[hp, core], g3_recv.at[z], dev(y, core, 4 * c + hp, x)
        )

    def g3_local(hp):
        return pltpu.make_async_copy(s2b.at[hp], r3.at[z], g3_recv.at[z])

    def send_grad(hp):
        for d in (2, 1, 3):
            for i in range(2):
                g1_copy(hp, i, d).start()

    def sum_first(hp):
        for i in range(2):
            arrived, own = (r1_a, r1_b)[i], (gf_a, gf_b)[i]
            total = own[hp, own_place(along_y(hp, i, 0))]
            for d in (1, 3, 2):
                wait_for(arrived.at[hp, d - 1], g1_recv.at[hp, i, d - 1])
                total = total + arrived[hp, d - 1].astype(F32)
            (s1f_a, s1f_b)[i][hp] = total
            (s1b_a, s1b_b)[i][hp] = total.astype(BF)
            for d in (2, 1, 3):
                g2_copy(hp, i, d).start()

    def sum_second(hp):
        totals = []
        for i in range(2):
            arrived = (r2_a, r2_b)[i]
            total = (s1f_a, s1f_b)[i][hp, own_place(along_y(hp, i, 1))]
            for d in (1, 3, 2):
                wait_for(arrived.at[hp, d - 1], g2_recv.at[hp, i, d - 1])
                total = total + arrived[hp, d - 1].astype(F32)
            totals.append(total.astype(BF))
        s2b[hp] = jnp.concatenate(totals, 1)
        for core in range(2):
            own = (4 * c + hp == z) & (c == core)
            pl.when(own)(lambda: g3_local(hp).start())
            pl.when(jnp.logical_not(own))(lambda: g3_copy(hp, core).start())

    def chunks(act):
        for r in range(ROWS // CHUNK):
            act(r, pl.ds(r * CHUNK, CHUNK))

    def both_heads(hp):
        keys_values(hp, 0)
        attend(hp)
        at_copy(hp).start()
        grad(hp)
        send_grad(hp)

    def slot(g, _):
        pl.when(g < PAIRS - 1)(lambda: send_own(g + 1))
        pl.when(g < PAIRS + 1)(lambda: pump_first(g - 1))
        pl.when((g >= 2) & (g < PAIRS + 2))(lambda: pump_second(g - 2))

        @pl.when(g == 3)
        def _():
            chunks(lambda r, rows: wait_for(acts.at[2 * oc + 1, rows], act_recv.at[0, r]))

        pl.when((g >= 3) & (g <= 5))(lambda: own_part(g - 3))

        @pl.when(g == 4)
        def _():
            def onward(r, rows):
                wait_for(acts.at[2 * c, rows], act_recv.at[1, r])
                act_pass(r).start()

            chunks(onward)
            chunks(lambda r, rows: wait_for(acts.at[2 * oc, rows], act_recv.at[2, r]))
            wait_for(lohi_b.at[oc], small_recv.at[0])
            wait_for(cot_sib, small_recv.at[1])

        pl.when(g >= 4)(lambda: both_heads(g - 4))
        pl.when(g >= 6)(lambda: sum_first(g - 6))
        pl.when(g >= 7)(lambda: sum_second(g - 7))
        pl.when(g == 6)(lambda: own_part(PAIRS - 1))
        return 0

    lax.fori_loop(1, PAIRS + 4, slot, 0)

    wo_copy.wait()
    small_eye = identity(ROWS)

    def project(part):
        total = None
        for hp in range(PAIRS):
            if part == 0:
                rows, core = at[hp, c], c
            else:
                rows, core = at_sib[hp], oc
            turned = dot_nt(small_eye, rows).astype(BF)
            start = pl.multiple_of(core * (PAIRS * UNIT) + hp * UNIT, UNIT)
            term = dot(turned, w_o_v[pl.ds(start, UNIT), :])
            total = term if total is None else total + term
        return total

    ext[0:ROWS] = project(0)
    sum_first(PAIRS - 2)
    sum_second(PAIRS - 3)
    sum_first(PAIRS - 1)
    sum_second(PAIRS - 2)
    for hp in range(PAIRS):
        wait_for(at_sib.at[hp], at_recv.at[hp])
    mixed[...] = (ext[0:ROWS] + project(1)).astype(BF)
    sum_second(PAIRS - 1)

    for v in range(NZ):
        wait_for(r3.at[v], g3_recv.at[v])
    total = r3[0].astype(F32)
    for v in range(1, NZ):
        total = total + r3[v].astype(F32)
    wgrad[...] = jnp.where(c == 0, total[:, :UNIT], total[:, UNIT:])

    up.wait_send()
    down.wait_send()
    lohi_copy.wait_send()
    cot_copy.wait_send()

    for j in range(3):
        for d in (2, 1, 3):
            to_y(j, d).wait_send()

        @pl.when(owned(j)[2] != c)
        def _(j=j):
            for e in range(4):
                to_sibling(j, e).wait_send()

    for r in range(ROWS // CHUNK):
        act_copy(0, r).wait_send()
        act_copy(1, r).wait_send()
        act_pass(r).wait_send()

    def sent_parts(hp, _):
        for t in range(3):
            idx, need = foreign(hp, t)

            @pl.when(need)
            def _(idx=idx, t=t):
                for i in range(3):
                    pass_copy(idx, t, i).wait_send()

        at_copy(hp).wait_send()
        return 0

    lax.fori_loop(0, PAIRS, sent_parts, 0)
    for hp in range(PAIRS):
        for i in range(2):
            for d in range(1, 4):
                g1_copy(hp, i, d).wait_send()
                g2_copy(hp, i, d).wait_send()
        for core in range(2):
            own = (4 * c + hp == z) & (c == core)
            pl.when(jnp.logical_not(own))(lambda: g3_copy(hp, core).wait_send())


def local(frames, seg, look_back, w_dw, w_qkv, w_o, cotangent):
    vmem, hbm = pl.BlockSpec(memory_space=pltpu.VMEM), pl.BlockSpec(memory_space=pl.ANY)
    dma = pltpu.SemaphoreType.DMA
    return pl.pallas_call(
        kernel,
        name="block",
        out_shape=(
            jax.ShapeDtypeStruct((ROWS, WIDTH), BF),
            jax.ShapeDtypeStruct((QUARTER, UNIT), F32),
        ),
        in_specs=[vmem, vmem, vmem, vmem, vmem, vmem, hbm],
        out_specs=(vmem, vmem),
        scratch_shapes=[
            pltpu.VMEM((3 * PAIRS, 4, QUARTER, WIDTH), BF),
            pltpu.VMEM((ROWS + 2 * EDGE, WIDTH), F32),
            pltpu.VMEM((2, EDGE, WIDTH), BF),
            pltpu.VMEM((ROWS + 2 * EDGE, 128), jnp.int32),
            pltpu.VMEM((KER, ROWS, 128), F32),
            pltpu.VMEM((4, ROWS, WIDTH), BF),
            pltpu.VMEM((2, 8, ROWS), jnp.int32),
            pltpu.VMEM((WIDTH, WIDTH), BF),
            pltpu.VMEM((ROWS, WIDTH), BF),
            pltpu.VMEM((PAIRS, 2, UNIT, ROWS), BF),
            pltpu.VMEM((PAIRS, 2, 2 * ROWS, UNIT), BF),
            pltpu.VMEM((PAIRS, 2, UNIT, 2 * ROWS), BF),
            pltpu.VMEM((PAIRS, 2, UNIT, ROWS), BF),
            pltpu.VMEM((PAIRS, UNIT, ROWS), BF),
            pltpu.VMEM((PAIRS, 4, 4, QUARTER, SPLIT), F32),
            pltpu.VMEM((PAIRS, 4, 4, QUARTER, COLS - SPLIT), F32),
            pltpu.VMEM((PAIRS, 4, 4, QUARTER, SPLIT), BF),
            pltpu.VMEM((PAIRS, 4, 4, QUARTER, COLS - SPLIT), BF),
            pltpu.VMEM((PAIRS, 3, 4, QUARTER, SPLIT), BF),
            pltpu.VMEM((PAIRS, 3, 4, QUARTER, COLS - SPLIT), BF),
            pltpu.VMEM((PAIRS, 4, QUARTER, SPLIT), F32),
            pltpu.VMEM((PAIRS, 4, QUARTER, COLS - SPLIT), F32),
            pltpu.VMEM((PAIRS, 4, QUARTER, SPLIT), BF),
            pltpu.VMEM((PAIRS, 4, QUARTER, COLS - SPLIT), BF),
            pltpu.VMEM((PAIRS, 3, QUARTER, SPLIT), BF),
            pltpu.VMEM((PAIRS, 3, QUARTER, COLS - SPLIT), BF),
            pltpu.VMEM((PAIRS, QUARTER, COLS), BF),
            pltpu.VMEM((NZ, QUARTER, COLS), BF),
            dma((3, 8)),
            dma((3 * PAIRS, 4)),
            dma((3 * PAIRS, 3)),
            dma((2,)),
            dma((2,)),
            dma((3, 4)),
            dma((3, 4)),
            dma((2,)),
            dma((2,)),
            dma((PAIRS,)),
            dma((PAIRS,)),
            dma((PAIRS, 2, 3)),
            dma((PAIRS, 2, 3)),
            dma((PAIRS, 2, 3)),
            dma((PAIRS, 2, 3)),
            dma((PAIRS, 2)),
            dma((NZ,)),
            dma,
        ],
        compiler_params=pltpu.CompilerParams(
            collective_id=0, has_side_effects=True, vmem_limit_bytes=58 * 2**20
        ),
        cost_estimate=pl.CostEstimate(flops=10**10, bytes_accessed=10**7, transcendentals=2 * 10**6),
    )(frames, seg, look_back, w_dw, w_qkv.T, cotangent, w_o)


def solution(mesh):
    placed = (
        P(("dp", "tm"), None),
        P("dp", None),
        P("dp", None),
        P(),
        P(None, "dp"),
        P(),
        P(("dp", "tm"), None),
    )
    return jax.shard_map(
        local,
        mesh=mesh,
        in_specs=placed,
        out_specs=(P(("dp", "tm"), None), P("tm", "dp")),
        check_vma=False,
    )
```
